256 devices in a mesh: gx: 16 (over z_lo, y), gy: 4 (over x), gz: 4 (over z_hi, core).
Axes of the slice: x: 4, y: 4, z: 8 (z_hi: 2, z_lo: 4; z = z_hi * 4 + z_lo), core: 2. Of those that a mesh axis runs over, the one named last changes fastest.
Arguments:
- displacement: float32 [3, 1024, 128, 512], P(None, 'gx', 'gy', 'gz'), as said below
- density: float32 [1024, 128, 512], P('gx', 'gy', 'gz'), may hold values from 0.1 to 0.9
- cell_flags: int32 [1024, 128, 512], P('gx', 'gy', 'gz'), may hold values from 0 to 2
- trim_level: int32 [1024, 128, 512], P('gx', 'gy', 'gz'), may hold values from 0 to 3
Outputs:
- projected: float32 [1024, 128, 512], P('gx', 'gy', 'gz')
- filtered: float32 [1024, 128, 512], P('gx', 'gy', 'gz')
The draws below stay inside these ranges and needn't reach their ends.
Inputs may be any that keep to these rules, and one draw needn't show every extreme that they name: `displacement`: displacements of order one.
All inputs are finite; a program needn't handle non-finite values.
Results may differ from the reference program's by a relative error of at most 0.0003.
Values sent between devices are 32-bit elements; how exact they have to be, the bound alone decides.
No kernel may reach another device: no remote copies, remote signals or barrier semaphores. Data moves between devices by JAX's collectives and lax.ppermute only.
A program may use at most 128 MiB of HBM per device.

```python
import math
import jax
import jax.numpy as jnp
from jax import lax

CX = 64
SWEEPS = 4
NX = 1024
NY = 128
NZ = 512


def draw_displacement(key, part):
    key = jax.random.fold_in(key, 11)
    position = lax.broadcasted_iota(jnp.float32, (3, NX, NY, NZ), 1)
    amplitude = 0.6 + 0.8 * position / max(NX - 1, 1)
    return jax.random.normal(key, (3, NX, NY, NZ), jnp.float32) * amplitude


def set_ends(values, rng, least, high):
    dims = values.shape
    place = [jax.random.randint(jax.random.fold_in(rng, axis), (), 0, dims[axis]) for axis in range(len(dims))]
    values = values.at[tuple(place)].set(least)
    longest = dims.index(max(dims))
    place[longest] = (place[longest] + 1) % dims[longest]
    return values.at[tuple(place)].set(high)


def block_levels(own_key, extent, cuts, low, top_value):
    level = 1.0
    for dim, blocks in cuts:
        steps = jax.random.uniform(jax.random.fold_in(jax.random.fold_in(own_key, 6), dim), (blocks,), jnp.float32, low / len(cuts), top_value / len(cuts))
        level = level * jnp.repeat(jnp.exp(steps), extent[dim] // blocks).reshape((-1,) + (1,) * (len(extent) - 1 - dim))
    return level


def setup_inputs(seed: int = 0) -> dict:
    key_list = jax.random.split(jax.random.key(seed), 5)
    return {
        "displacement": draw_displacement(jax.random.fold_in(key_list[4], 71), 0),
        "density": jnp.clip(0.1 + 0.79999997 * jax.random.uniform(key_list[1], (NX, NY, NZ), jnp.float32) ** block_levels(key_list[1], (NX, NY, NZ), ((0, 16), (1, 4), (2, 4)), -0.2, 0.2), 0.1, 0.9),
        "cell_flags": set_ends(jax.random.randint(key_list[2], (NX, NY, NZ), 0, 3), jax.random.fold_in(key_list[2], 1), 0, 2).astype(jnp.int32),
        "trim_level": set_ends(jax.random.randint(key_list[3], (NX, NY, NZ), 0, 4), jax.random.fold_in(key_list[3], 1), 0, 3).astype(jnp.int32),
    }


LAMBDA = 0.3 / 0.52
SHEAR_MODULUS = 1.0 / 2.6
FILTER_COEF = 0.75
SPREAD_MID = 5.5
SPREAD_HALF = 4.5
STEP_SIZE = 0.3
SHARPNESS = 8.0
THRESHOLD = 0.5
GAUSS_POINTS = [0.5 - 0.5 / math.sqrt(3.0), 0.5 + 0.5 / math.sqrt(3.0)]
VALUES = [[(1.0 - t) ** 2 / 2.0, (1.0 + 2.0 * t - 2.0 * t * t) / 2.0, t * t / 2.0] for t in GAUSS_POINTS]
SLOPES = [[t - 1.0, 1.0 - 2.0 * t, t] for t in GAUSS_POINTS]

def spline_pass(field, axis, weights):
    length = field.shape[axis] - 2
    total = weights[0] * lax.slice_in_dim(field, 0, length, axis=axis)
    total = total + weights[1] * lax.slice_in_dim(field, 1, length + 1, axis=axis)
    return total + weights[2] * lax.slice_in_dim(field, 2, length + 2, axis=axis)

def point_energy(grads):
    trace = grads[0][0] + grads[1][1] + grads[2][2]
    squares = grads[0][0] ** 2 + grads[1][1] ** 2 + grads[2][2] ** 2
    squares = squares + 0.5 * ((grads[0][1] + grads[1][0]) ** 2 + (grads[0][2] + grads[2][0]) ** 2 + (grads[1][2] + grads[2][1]) ** 2)
    return LAMBDA * trace * trace + 2.0 * SHEAR_MODULUS * squares

def strain_energy(padded):
    along_z = [[(spline_pass(padded[component], 2, VALUES[point]), spline_pass(padded[component], 2, SLOPES[point])) for point in range(2)] for component in range(3)]
    total = 0.0
    for point_z in range(2):
        for point_y in range(2):
            partial_y = []
            for component in range(3):
                value_z, slope_z = along_z[component][point_z]
                partial_y.append((spline_pass(value_z, 1, VALUES[point_y]), spline_pass(value_z, 1, SLOPES[point_y]), spline_pass(slope_z, 1, VALUES[point_y])))
            for point_x in range(2):
                grads = []
                for component in range(3):
                    plain, slope_y, slope_zz = partial_y[component]
                    grads.append((spline_pass(plain, 0, SLOPES[point_x]), spline_pass(slope_y, 0, VALUES[point_x]), spline_pass(slope_zz, 0, VALUES[point_x])))
                total = total + point_energy(grads)
    return total * 0.125

def cell_source(energy, density, cell_flags, trim_level):
    trimmed = (1.0 + trim_level.astype(jnp.float32)) / 5.0
    share = jnp.where(cell_flags == 1, 1.0, jnp.where(cell_flags == 2, trimmed, 0.001)).astype(jnp.float32)
    return -3.0 * density * density * density * share * energy

def stencil(padded):
    center = padded[1:-1, 1:-1, 1:-1]
    beside = padded[2:, 1:-1, 1:-1] + padded[:-2, 1:-1, 1:-1]
    beside = beside + padded[1:-1, 2:, 1:-1] + padded[1:-1, :-2, 1:-1]
    beside = beside + padded[1:-1, 1:-1, 2:] + padded[1:-1, 1:-1, :-2]
    return (1.0 + 6.0 * FILTER_COEF) * center - FILTER_COEF * beside

def chebyshev(source, apply_fn):
    sigma = SPREAD_MID / SPREAD_HALF
    solution = jnp.zeros_like(source)
    residual = source
    direction = source / SPREAD_MID
    rho_old = 1.0 / sigma
    for sweep_index in range(SWEEPS):
        image = apply_fn(direction)
        solution = solution + direction
        residual = residual - image
        rho_new = 1.0 / (2.0 * sigma - rho_old)
        direction = rho_new * rho_old * direction + 2.0 * rho_new / SPREAD_HALF * residual
        rho_old = rho_new
    return solution + direction

def projection(density, filtered, scale):
    trial = density - STEP_SIZE * (filtered / scale + 1.0)
    lower = math.tanh(SHARPNESS * THRESHOLD)
    return (lower + jnp.tanh(SHARPNESS * (trial - THRESHOLD))) / (lower + math.tanh(SHARPNESS * (1.0 - THRESHOLD)))

def reference(displacement, density, cell_flags, trim_level):
    padded_all = jnp.pad(displacement, ((0, 0), (1, 1), (1, 1), (1, 1)))

    def one_block(block_index):
        start = (block_index * CX).astype(jnp.int32)
        block = lax.dynamic_slice_in_dim(padded_all, start, CX + 2, 1)
        return strain_energy(block)
    energy = lax.map(one_block, jnp.arange(NX // CX, dtype=jnp.int32)).reshape(NX, NY, NZ)
    source = cell_source(energy, density, cell_flags, trim_level)

    def apply_whole(direction):
        return stencil(jnp.pad(direction, 1))
    filtered = chebyshev(source, apply_whole)
    scale = jnp.sum(jnp.abs(filtered)) / (NX * NY * NZ) + 1e-06
    return (projection(density, filtered, scale), filtered)
```

```python
import functools
import math

import jax
import jax.numpy as jnp
from jax import lax
from jax.experimental import pallas as pl
from jax.experimental.pallas import tpu as pltpu
from jax.sharding import PartitionSpec as P

LAMBDA = 0.3 / 0.52
SHEAR_MODULUS = 1.0 / 2.6
SPREAD_MID = 5.5
SPREAD_HALF = 4.5
STEP_SIZE = 0.3
SHARPNESS = 8.0
THRESHOLD = 0.5

AXES = ("gx", "gy", "gz")
LANES = 128
REACH = 4
WIDE = REACH + 1

SIGMA = SPREAD_MID / SPREAD_HALF
CHEB = 16.0 * SIGMA**5 - 20.0 * SIGMA**3 + 5.0 * SIGMA
POLY = [
    (16.0 * SIGMA**4 - 20.0 * SIGMA**2 + 5.0) / (SPREAD_HALF * CHEB),
    (16.0 * SIGMA**3 - 20.0 * SIGMA) / 6.0 / (SPREAD_HALF * CHEB),
    (16.0 * SIGMA**2 - 20.0) / 36.0 / (SPREAD_HALF * CHEB),
    16.0 * SIGMA / 216.0 / (SPREAD_HALF * CHEB),
    16.0 / 1296.0 / (SPREAD_HALF * CHEB),
]

F32 = jnp.float32
VMEM = pl.BlockSpec(memory_space=pltpu.VMEM)
PARAMS = dict(vmem_limit_bytes=56 * 1024 * 1024)


def swap(first, second, axis):
    count = lax.axis_size(axis)
    even = [(i, i ^ 1) for i in range(count)]
    odd = [(i, i + 1 if i % 2 else i - 1) for i in range(1, count - 1)]
    got_first = lax.ppermute(first, axis, even)
    got_second = lax.ppermute(second, axis, odd) if odd else jnp.zeros_like(second)
    return got_first, got_second


def is_odd(axis):
    return lax.rem(lax.axis_index(axis), 2) == 1


def cell_coef(density, cell_flags, trim_level):
    trimmed = (1.0 + trim_level.astype(F32)) * 0.2
    share = jnp.where(cell_flags == 1, 1.0, jnp.where(cell_flags == 2, trimmed, 0.001))
    return -3.0 * density * density * density * share


def lane_ids():
    return lax.broadcasted_iota(jnp.int32, (8, LANES), 1)


def row_ids():
    return lax.broadcasted_iota(jnp.int32, (8, LANES), 0)


def half_turn(tile):
    return pltpu.roll(tile, 4, 0)


def rim_tile(first, second, index, odd):
    one = jnp.broadcast_to(first[pl.ds(index, 1), :], (8, LANES))
    two = jnp.broadcast_to(second[pl.ds(index, 1), :], (8, LANES))
    at_top = row_ids() == 0
    return jnp.where(jnp.logical_xor(at_top, odd), one, two)


def ends_kernel(disp, xr1, xr2, yr1, yr2, zs1, zs2):
    _, bx, by, _ = disp.shape
    planes = bx + 2 * WIDE
    odd_y, odd_z = is_odd("gy"), is_odd("gz")
    lane = lane_ids()

    def gather(tile_of, c, row):
        low = jnp.zeros((8, LANES), F32)
        high = jnp.zeros((8, LANES), F32)
        for x in range(planes):
            tile = tile_of(x)
            here = lane == x
            low = jnp.where(here, pltpu.roll(tile, x, 1) if x else tile, low)
            high = jnp.where(here, pltpu.roll(tile, x + 1, 1), high)
        zs1[c, pl.ds(row, 8), :] = jnp.where(odd_z, low, high)
        zs2[c, pl.ds(row, 8), :] = jnp.where(odd_z, high, low)

    for c in range(3):

        def rows(t, carry, c=c):
            row = pl.multiple_of(8 * t, 8)

            def tile_of(x):
                if x < WIDE:
                    return xr1[c * WIDE + x, pl.ds(row, 8), :]
                if x < WIDE + bx:
                    return disp[c, x - WIDE, pl.ds(row, 8), :]
                return xr2[c * WIDE + x - WIDE - bx, pl.ds(row, 8), :]

            gather(tile_of, c, row)
            return carry

        lax.fori_loop(0, by // 8, rows, 0)
        gather(lambda x, c=c: rim_tile(yr1, yr2, c * planes + x, odd_y), c, by)


def triple(a, b, c):
    ends = a + c
    curve = ends - 2.0 * b
    return 4.0 * b + (2.0 / 3.0) * curve, c - a, curve


def pair(a, b, c):
    return (2.0 / 3.0) * (a + c) + (8.0 / 3.0) * b, c - a


def energy_of(fields):
    grads = []
    for c in range(3):
        g = {}
        for key, planes in fields[c].items():
            if key == "MM":
                a, b, n = planes
                g["DMM"], g["SMM"] = n - a, (a + n) - 2.0 * b
            elif key in ("MD", "DM", "DD"):
                g["M" + key], g["D" + key], g["S" + key] = triple(*planes)
            else:
                g["M" + key], g["D" + key] = pair(*planes)
        grads.append(g)
    names = "MD", "DS"

    def part(c, e, p):
        return grads[c]["".join(names[1 if d == e else 0][p[d]] for d in range(3))]

    traces = normals = shears = None
    for order in (3, 2, 1, 0):
        if traces is not None:
            traces, normals, shears = (v * (1.0 / 3.0) for v in (traces, normals, shears))
        for bits in range(8):
            p = (bits >> 2) & 1, (bits >> 1) & 1, bits & 1
            if sum(p) != order:
                continue
            xx, yy, zz = (part(c, c, p) for c in range(3))
            xy = part(0, 1, p) + part(1, 0, p)
            xz = part(0, 2, p) + part(2, 0, p)
            yz = part(1, 2, p) + part(2, 1, p)
            trace = xx + yy + zz
            trace = trace * trace
            normal = xx * xx + yy * yy + zz * zz
            shear = xy * xy + xz * xz + yz * yz
            if traces is None:
                traces, normals, shears = trace, normal, shear
            else:
                traces, normals, shears = traces + trace, normals + normal, shears + shear
    scale = 1.0 / 1024.0
    return (
        (LAMBDA * scale) * traces
        + (2.0 * SHEAR_MODULUS * scale) * normals
        + (SHEAR_MODULUS * scale) * shears
    )


YZ = ("MM", "MD", "MS", "DM", "DD", "DS", "SM", "SD")


def source_kernel(
    disp, density, flags, trim, xr1, xr2, yr1, yr2, zr1, zr2,
    source, ys1, ys2, packed,
    field, coef, zlow, zhigh, along, ring,
):
    _, bx, by, _ = disp.shape
    planes = bx + 2 * WIDE
    cells = bx + 2 * REACH
    odd_x, odd_y, odd_z = is_odd("gx"), is_odd("gy"), is_odd("gz")
    lane, row = lane_ids(), row_ids()

    for k in range(WIDE):
        for c in range(3):
            field[c, jnp.where(odd_x, 0, bx + WIDE) + k, 0:by, :] = xr1[c * WIDE + k]
            field[c, jnp.where(odd_x, bx + WIDE, 0) + k, 0:by, :] = xr2[c * WIDE + k]
    for k in range(REACH):
        coef[jnp.where(odd_x, 0, bx + REACH) + k] = xr1[3 * WIDE + k]
        coef[jnp.where(odd_x, bx + REACH, 0) + k] = xr2[3 * WIDE + k]

    def fill(x, carry):
        for c in range(3):
            field[c, x + WIDE, 0:by, :] = disp[c, x]
        coef[x + REACH] = cell_coef(density[x], flags[x], trim[x])
        return carry

    lax.fori_loop(0, bx, fill, 0)

    def place(x):
        low = jnp.where(x < WIDE, x + bx + WIDE, x)
        swapped = jnp.where(x >= bx + WIDE, x - bx - WIDE, low)
        return jnp.where(odd_x, x, swapped)

    def rim(x, carry):
        for c in range(3):
            field[c, x, by : by + 8, :] = rim_tile(yr1, yr2, c * planes + place(x), odd_y)
        return carry

    lax.fori_loop(0, planes, rim, 0)
    zlow[...] = jnp.where(odd_z, zr1[...], zr2[...])
    zhigh[...] = jnp.where(odd_z, zr2[...], zr1[...])

    def plane(x, slot):
        spot = place(x)
        to_first = lax.rem(LANES - spot, LANES)
        to_last = LANES - 1 - spot
        for c in range(3):
            for t in range(by // 8 + 1):
                rows = slice(8 * t, 8 * t + 8)
                mid = field[c, x, rows, :]
                low = pltpu.roll(zlow[c, rows, :], to_first, 1)
                high = pltpu.roll(zhigh[c, rows, :], to_last, 1)
                low = jnp.where(lane == 0, low, pltpu.roll(mid, 1, 1))
                high = jnp.where(lane == LANES - 1, high, pltpu.roll(mid, LANES - 1, 1))
                for k, v in enumerate(triple(low, mid, high)):
                    along[3 * c + k, 8 * t + 8 : 8 * t + 16, :] = v
                    if t == by // 8:
                        along[3 * c + k, 0:8, :] = v
        at = jnp.maximum(x - 2, 0)
        for t in range(by // 8):
            rows = slice(8 * t, 8 * t + 8)
            fields = []
            for c in range(3):
                now = {}
                for k, z in enumerate("MDS"):
                    three = [along[3 * c + k, 8 * t + 7 + o : 8 * t + 15 + o, :] for o in range(3)]
                    if z == "S":
                        now["MS"], now["DS"] = pair(*three)
                    else:
                        now["M" + z], now["D" + z], now["S" + z] = triple(*three)
                held = {}
                for k, key in enumerate(YZ):
                    f = 8 * c + k
                    held[key] = ring[slot, f, rows, :], ring[1 - slot, f, rows, :], now[key]
                for k, key in enumerate(YZ):
                    ring[slot, 8 * c + k, rows, :] = now[key]
                fields.append(held)
            source[at, rows, :] = coef[at, rows, :] * energy_of(fields)

    def planes_two(k, carry):
        plane(2 * k, 0)
        plane(2 * k + 1, 1)
        return carry

    lax.fori_loop(0, planes // 2, planes_two, 0)

    def rows_out(q, carry):
        top = row < 4
        first, second = source[2 * q, 0:8, :], source[2 * q + 1, 0:8, :]
        low = jnp.where(top, first, half_turn(second))
        first, second = source[2 * q, by - 8 : by, :], source[2 * q + 1, by - 8 : by, :]
        high = jnp.where(top, half_turn(first), second)
        ys1[q] = jnp.where(odd_y, low, high)
        ys2[q] = jnp.where(odd_y, high, low)
        return carry

    lax.fori_loop(0, cells // 2, rows_out, 0)
    pack_columns(source, packed, by)


def pack_columns(source, packed, count):
    cells = source.shape[0]
    row = row_ids()
    for y in range(count):
        tall = jnp.concatenate([source[:, y, :], jnp.zeros((LANES - cells, LANES), F32)], axis=0)
        flat = tall.T
        packed[y] = jnp.where(row < 4, flat[0:8], flat[LANES - 8 : LANES])


def corner_kernel(yr1, yr2, packed, rim, rim_packed, zs1, zs2):
    by = packed.shape[0]
    odd_y, odd_z = is_odd("gy"), is_odd("gz")
    top = row_ids() < 4

    def unpack(q, carry):
        high = jnp.where(odd_y, yr2[q], yr1[q])
        low = jnp.where(odd_y, yr1[q], yr2[q])
        rim[2 * q] = jnp.where(top, high, half_turn(low))
        rim[2 * q + 1] = jnp.where(top, half_turn(high), low)
        return carry

    lax.fori_loop(0, yr1.shape[0], unpack, 0)
    pack_columns(rim, rim_packed, 8)

    def send(m, first, second):
        low = jnp.where(top, first, half_turn(second))
        high = jnp.where(top, half_turn(first), second)
        zs1[m] = jnp.where(odd_z, low, high)
        zs2[m] = jnp.where(odd_z, high, low)

    for m in range(by // 2):
        send(m, packed[2 * m], packed[2 * m + 1])
    for m in range(4):
        send(by // 2 + m, rim_packed[2 * m], rim_packed[2 * m + 1])


def filter_kernel(
    source, rim, packed, rim_packed, zr1, zr2, filtered, partial,
    work, low_strip, high_strip, strips, ends,
):
    cells, by, _ = source.shape
    bx = cells - 2 * REACH
    tall = by + 8
    odd_z = is_odd("gz")
    lane, row = lane_ids(), row_ids()
    top = row < 4
    first_x, last_x = lax.axis_index("gx") == 0, lax.axis_index("gx") == lax.axis_size("gx") - 1
    first_y, last_y = lax.axis_index("gy") == 0, lax.axis_index("gy") == lax.axis_size("gy") - 1
    first_z, last_z = lax.axis_index("gz") == 0, lax.axis_index("gz") == lax.axis_size("gz") - 1

    for m in range(tall // 2):
        low = jnp.where(odd_z, zr1[m], zr2[m])
        high = jnp.where(odd_z, zr2[m], zr1[m])
        for part in range(2):
            y = 2 * m + part
            own = half_turn(packed[y] if y < by else rim_packed[y - by])
            low_strip[y] = jnp.where(top, half_turn(low) if part else low, own)
            high_strip[y] = jnp.where(top, own, high if part else half_turn(high))

    inside_x = jnp.logical_not(
        jnp.logical_or(
            jnp.logical_and(first_x, lane < REACH),
            jnp.logical_and(last_x, lane >= bx + REACH),
        )
    )
    inside_low = jnp.logical_and(inside_x, jnp.logical_not(jnp.logical_and(first_z, top)))
    inside_high = jnp.logical_and(
        inside_x, jnp.logical_not(jnp.logical_and(last_z, jnp.logical_not(top)))
    )
    for side, strip, edge_row, inside in (
        (0, low_strip, 3, inside_low),
        (1, high_strip, 4, inside_high),
    ):
        strips[0] = POLY[4] * strip[...]
        for k in range(4):
            now, later = k % 2, (k + 1) % 2
            for t in range(tall // 8):
                ends[k, side, 8 * t : 8 * t + 8, :] = strips[now, 8 * t : 8 * t + 8, edge_row, :]
            if k == 3:
                break
            for y in range(tall):
                mid = strips[now, y]
                total = strips[now, (y + 1) % tall] + strips[now, (y - 1) % tall]
                total = total + (pltpu.roll(mid, 1, 1) + pltpu.roll(mid, LANES - 1, 1))
                total = total + (pltpu.roll(mid, 1, 0) + pltpu.roll(mid, 7, 0))
                total = total + POLY[3 - k] * strip[y]
                outside = first_y if y >= by + 4 else last_y
                keep = inside
                if y >= by:
                    keep = jnp.logical_and(inside, jnp.logical_not(outside))
                strips[later, y] = jnp.where(keep, total, 0.0)

    def put(slot, x, t, value):
        work[slot, x, 8 * t + 8 : 8 * t + 16, :] = value
        if t == by // 8:
            work[slot, x, 0:8, :] = value
        if t == 0:
            work[slot, x, by + 16 : by + 24, :] = value

    def begin(x, carry):
        for t in range(by // 8):
            put(0, x, t, POLY[4] * source[x, 8 * t : 8 * t + 8, :])
        put(0, x, by // 8, POLY[4] * rim[x])
        return carry

    lax.fori_loop(0, cells, begin, 0)
    rim_keep = jnp.logical_not(
        jnp.logical_or(
            jnp.logical_and(last_y, top), jnp.logical_and(first_y, jnp.logical_not(top))
        )
    )
    tiles = by // 8
    for k in range(4):
        now, later = k % 2, (k + 1) % 2

        def sweep(x, total, k=k, now=now, later=later):
            to_first = lax.rem(LANES - x, LANES)
            to_last = LANES - 1 - x
            for t in range(tiles + (k < 3)):
                at = 8 * t + 8
                mid = work[now, x, at : at + 8, :]
                value = work[now, x - 1, at : at + 8, :] + work[now, x + 1, at : at + 8, :]
                value = value + (
                    work[now, x, at - 1 : at + 7, :] + work[now, x, at + 1 : at + 9, :]
                )
                low = pltpu.roll(ends[k, 0, 8 * t : 8 * t + 8, :], to_first, 1)
                high = pltpu.roll(ends[k, 1, 8 * t : 8 * t + 8, :], to_last, 1)
                low = jnp.where(lane == 0, low, pltpu.roll(mid, 1, 1))
                high = jnp.where(lane == LANES - 1, high, pltpu.roll(mid, LANES - 1, 1))
                value = value + (low + high)
                own = source[x, 8 * t : 8 * t + 8, :] if t < tiles else rim[x]
                value = value + POLY[3 - k] * own
                if k == 3:
                    filtered[x - REACH, 8 * t : 8 * t + 8, :] = value
                    total = total + jnp.abs(value)
                else:
                    if t == tiles:
                        value = jnp.where(rim_keep, value, 0.0)
                    put(later, x, t, value)
            return total

        total = lax.fori_loop(k + 1, cells - 1 - k, sweep, jnp.zeros((8, LANES), F32))
        if k < 3:

            @pl.when(first_x)
            def _(later=later):
                work[later, 0:REACH] = jnp.zeros((REACH,) + work.shape[2:], F32)

            @pl.when(last_x)
            def _(later=later):
                work[later, bx + REACH : cells] = jnp.zeros((REACH,) + work.shape[2:], F32)

    partial[...] = jnp.broadcast_to(jnp.sum(total, axis=0, keepdims=True), partial.shape)


def project_kernel(count, density, filtered, sums, projected):
    scale = jnp.sum(sums[...]) / count + 1e-06
    inverse = jnp.full((8, LANES), 1.0, F32) / scale
    lower = math.tanh(SHARPNESS * THRESHOLD)
    bottom = lower + math.tanh(SHARPNESS * (1.0 - THRESHOLD))

    def one(x, carry):
        for t in range(density.shape[1] // 8):
            rows = slice(8 * t, 8 * t + 8)
            trial = density[x, rows, :] - STEP_SIZE * (filtered[x, rows, :] * inverse + 1.0)
            level = lower + jnp.tanh(SHARPNESS * (trial - THRESHOLD))
            projected[x, rows, :] = level * (1.0 / bottom)
        return carry

    lax.fori_loop(0, density.shape[0], one, 0)


def call(kernel, outs, scratch=()):
    return pl.pallas_call(
        kernel,
        out_shape=[jax.ShapeDtypeStruct(s, F32) for s in outs],
        out_specs=[VMEM] * len(outs),
        scratch_shapes=[pltpu.VMEM(s, F32) for s in scratch],
        compiler_params=pltpu.CompilerParams(**PARAMS),
    )


def body(displacement, density, cell_flags, trim_level):
    bx, by, bz = density.shape
    assert bz == LANES and bx + 2 * WIDE <= LANES
    planes, cells, tall = bx + 2 * WIDE, bx + 2 * REACH, by + 8

    odd_x, odd_y = is_odd("gx"), is_odd("gy")

    def x_face(at_low):
        start = jnp.where(at_low, 0, bx - WIDE)
        near = lax.dynamic_slice_in_dim(displacement, start, WIDE, 1)
        start = jnp.where(at_low, 0, bx - REACH)
        near_coef = cell_coef(
            *(lax.dynamic_slice_in_dim(v, start, REACH, 0) for v in (density, cell_flags, trim_level))
        )
        return jnp.concatenate([near.reshape(3 * WIDE, by, bz), near_coef], axis=0)

    xr1, xr2 = swap(x_face(odd_x), x_face(jnp.logical_not(odd_x)), "gx")

    def y_face(at_low):
        start = jnp.where(at_low, 0, by - 1)
        parts = [xr1[: 3 * WIDE].reshape(3, WIDE, by, bz), displacement]
        parts.append(xr2[: 3 * WIDE].reshape(3, WIDE, by, bz))
        parts = [lax.dynamic_slice_in_dim(p, start, 1, 2)[:, :, 0, :] for p in parts]
        return jnp.concatenate(parts, axis=1).reshape(3 * planes, bz)

    yr1, yr2 = swap(y_face(odd_y), y_face(jnp.logical_not(odd_y)), "gy")
    zs1, zs2 = call(ends_kernel, [(3, tall, LANES)] * 2)(displacement, xr1, xr2, yr1, yr2)
    zr1, zr2 = swap(zs1, zs2, "gz")
    source, ys1, ys2, packed = call(
        source_kernel,
        [(cells, by, LANES), (cells // 2, 8, LANES), (cells // 2, 8, LANES), (by, 8, LANES)],
        [
            (3, planes, tall, LANES),
            (cells, by, LANES),
            (3, tall, LANES),
            (3, tall, LANES),
            (9, by + 16, LANES),
            (2, 24, by, LANES),
        ],
    )(displacement, density, cell_flags, trim_level, xr1, xr2, yr1, yr2, zr1, zr2)
    yr1, yr2 = swap(ys1, ys2, "gy")
    rim, rim_packed, zs1, zs2 = call(
        corner_kernel,
        [(cells, 8, LANES), (8, 8, LANES), (tall // 2, 8, LANES), (tall // 2, 8, LANES)],
    )(yr1, yr2, packed)
    zr1, zr2 = swap(zs1, zs2, "gz")
    devices = lax.axis_size(AXES)
    filtered, partial = call(
        filter_kernel,
        [(bx, by, LANES), (devices, LANES)],
        [
            (2, cells, by + 24, LANES),
            (tall, 8, LANES),
            (tall, 8, LANES),
            (2, tall, 8, LANES),
            (4, 2, tall, LANES),
        ],
    )(source, rim, packed, rim_packed, zr1, zr2)
    sums = lax.all_to_all(partial, AXES, split_axis=0, concat_axis=0, tiled=True)
    count = float(filtered.size * devices)
    (projected,) = call(functools.partial(project_kernel, count), [(bx, by, LANES)])(
        density, filtered, sums
    )
    return projected, filtered


def solution(mesh):
    return jax.shard_map(
        body,
        mesh=mesh,
        in_specs=(P(None, *AXES), P(*AXES), P(*AXES), P(*AXES)),
        out_specs=(P(*AXES), P(*AXES)),
        check_vma=False,
    )
```

```python
import functools
import math

import jax
import jax.numpy as jnp
from jax import lax
from jax.experimental import pallas as pl
from jax.experimental.pallas import tpu as pltpu
from jax.sharding import PartitionSpec as P

LAMBDA = 0.3 / 0.52
SHEAR_MODULUS = 1.0 / 2.6
SPREAD_MID = 5.5
SPREAD_HALF = 4.5
STEP_SIZE = 0.3
SHARPNESS = 8.0
THRESHOLD = 0.5

AXES = ("gx", "gy", "gz")
LANES = 128
HALF = 64
REACH = 4
WIDE = REACH + 1

SIGMA = SPREAD_MID / SPREAD_HALF
CHEB = 16.0 * SIGMA**5 - 20.0 * SIGMA**3 + 5.0 * SIGMA
POLY = [
    (16.0 * SIGMA**4 - 20.0 * SIGMA**2 + 5.0) / (SPREAD_HALF * CHEB),
    (16.0 * SIGMA**3 - 20.0 * SIGMA) / 6.0 / (SPREAD_HALF * CHEB),
    (16.0 * SIGMA**2 - 20.0) / 36.0 / (SPREAD_HALF * CHEB),
    16.0 * SIGMA / 216.0 / (SPREAD_HALF * CHEB),
    16.0 / 1296.0 / (SPREAD_HALF * CHEB),
]

F32 = jnp.float32
VMEM = pl.BlockSpec(memory_space=pltpu.VMEM)
PARAMS = dict(vmem_limit_bytes=20 * 1024 * 1024)


def swap(first, second, axis):
    count = lax.axis_size(axis)
    even = [(i, i ^ 1) for i in range(count)]
    odd = [(i, i + 1 if i % 2 else i - 1) for i in range(1, count - 1)]
    got_first = lax.ppermute(first, axis, even)
    got_second = lax.ppermute(second, axis, odd) if odd else jnp.zeros_like(second)
    return got_first, got_second


def is_odd(axis):
    return lax.rem(lax.axis_index(axis), 2) == 1


def cell_coef(density, cell_flags, trim_level):
    trimmed = (1.0 + trim_level.astype(F32)) * 0.2
    share = jnp.where(cell_flags == 1, 1.0, jnp.where(cell_flags == 2, trimmed, 0.001))
    return -3.0 * density * density * density * share


def lane_ids():
    return lax.broadcasted_iota(jnp.int32, (8, LANES), 1)


def row_ids():
    return lax.broadcasted_iota(jnp.int32, (8, LANES), 0)


def half_turn(tile):
    return pltpu.roll(tile, 4, 0)


def rim_tile(first, second, index, odd):
    one = jnp.broadcast_to(first[pl.ds(index, 1), :], (8, LANES))
    two = jnp.broadcast_to(second[pl.ds(index, 1), :], (8, LANES))
    at_top = row_ids() == 0
    return jnp.where(jnp.logical_xor(at_top, odd), one, two)


def two_halves(first, second):
    spare = HALF - first.shape[0]
    if spare:
        zero = jnp.zeros((spare, LANES), F32)
        first = jnp.concatenate([first, zero], axis=0)
        second = jnp.concatenate([second, zero], axis=0)
    return jnp.concatenate([first, second], axis=0).T


def faces_kernel(disp, low, high):
    _, _, by, _ = disp.shape
    n = by // 16
    for c in range(3):
        for y in range(by // 2):
            turned = two_halves(disp[c, :, y, :], disp[c, :, y + by // 2, :])
            low[c * n + y // 8, y % 8 : y % 8 + 1, :] = turned[0:1]
            high[c * n + y // 8, y % 8 : y % 8 + 1, :] = turned[LANES - 1 : LANES]


def ends_kernel(low, high, yr1, yr2, zs1, zs2):
    odd_z = is_odd("gz")
    n, bx = low.shape[0], yr1.shape[0] // 3
    zs1[0:n] = jnp.where(odd_z, low[...], high[...])
    zs2[0:n] = jnp.where(odd_z, high[...], low[...])
    zs1[n] = jnp.zeros((8, LANES), F32)
    zs2[n] = jnp.zeros((8, LANES), F32)
    for c in range(3):
        rows = slice(c * bx, c * bx + bx)
        turned = two_halves(yr1[rows, :], yr2[rows, :])
        near, far = turned[0:1], turned[LANES - 1 : LANES]
        zs1[n, c : c + 1, :] = jnp.where(odd_z, near, far)
        zs2[n, c : c + 1, :] = jnp.where(odd_z, far, near)


def x_rows(by):
    tall = by + 8
    planes = 3 * WIDE * tall
    coefs = planes + REACH * by
    return planes, coefs, coefs + 2 * 3 * (by // 16 + 1) * 8


def ends_tiles(by):
    return 3 * (by // 16 + 1)


def outward_kernel(disp, density, flags, trim, yr1, yr2, zr1, zr2, xs1, xs2, rims):
    _, bx, by, _ = disp.shape
    tall, n = by + 8, by // 16
    odd_x, odd_y, odd_z = is_odd("gx"), is_odd("gy"), is_odd("gz")
    top_row, left = row_ids() == 0, lane_ids() < HALF
    for side in range(2):
        def pick(*at, side=side):
            one, two = zr1[at], zr2[at]
            return jnp.where(odd_z, two, one) if side else jnp.where(odd_z, one, two)

        for c in range(3):
            base = side * ends_tiles(by) + c * (n + 1)
            for t in range(n):
                rims[base + t] = pick(c * n + t)
            both = jnp.broadcast_to(pick(3 * n, slice(c, c + 1), slice(None)), (8, LANES))
            other = pltpu.roll(both, HALF, 1)
            rims[base + n] = jnp.where(jnp.logical_xor(top_row, odd_y), both, other)
    planes, coefs, _ = x_rows(by)
    for out, at_low in ((xs1, odd_x), (xs2, jnp.logical_not(odd_x))):
        start = jnp.where(at_low, 0, bx - WIDE)
        for c in range(3):
            for k in range(WIDE):
                at = (c * WIDE + k) * tall
                out[at : at + by, :] = disp[c, start + k]
                out[at + by : at + tall, :] = rim_tile(yr1, yr2, c * bx + start + k, odd_y)
        start = jnp.where(at_low, 0, bx - REACH)
        for k in range(REACH):
            x = start + k
            out[planes + k * by : planes + (k + 1) * by, :] = cell_coef(density[x], flags[x], trim[x])
        for j in range(2 * ends_tiles(by)):
            out[coefs + 8 * j : coefs + 8 * j + 8, :] = rims[j]


def triple(a, b, c):
    ends = a + c
    curve = ends - 2.0 * b
    return 4.0 * b + (2.0 / 3.0) * curve, c - a, curve


def pair(a, b, c):
    return (2.0 / 3.0) * (a + c) + (8.0 / 3.0) * b, c - a


def energy_of(fields):
    grads = []
    for c in range(3):
        g = {}
        for key, planes in fields[c].items():
            if key == "MM":
                a, b, n = planes
                g["DMM"], g["SMM"] = n - a, (a + n) - 2.0 * b
            elif key in ("MD", "DM", "DD"):
                g["M" + key], g["D" + key], g["S" + key] = triple(*planes)
            else:
                g["M" + key], g["D" + key] = pair(*planes)
        grads.append(g)
    names = "MD", "DS"

    def part(c, e, p):
        return grads[c]["".join(names[1 if d == e else 0][p[d]] for d in range(3))]

    traces = normals = shears = None
    for order in (3, 2, 1, 0):
        if traces is not None:
            traces, normals, shears = (v * (1.0 / 3.0) for v in (traces, normals, shears))
        for bits in range(8):
            p = (bits >> 2) & 1, (bits >> 1) & 1, bits & 1
            if sum(p) != order:
                continue
            xx, yy, zz = (part(c, c, p) for c in range(3))
            xy = part(0, 1, p) + part(1, 0, p)
            xz = part(0, 2, p) + part(2, 0, p)
            yz = part(1, 2, p) + part(2, 1, p)
            trace = xx + yy + zz
            trace = trace * trace
            normal = xx * xx + yy * yy + zz * zz
            shear = xy * xy + xz * xz + yz * yz
            if traces is None:
                traces, normals, shears = trace, normal, shear
            else:
                traces, normals, shears = traces + trace, normals + normal, shears + shear
    scale = 1.0 / 1024.0
    return (
        (LAMBDA * scale) * traces
        + (2.0 * SHEAR_MODULUS * scale) * normals
        + (SHEAR_MODULUS * scale) * shears
    )


YZ = ("MM", "MD", "MS", "DM", "DD", "DS", "SM", "SD")


def z_pass(tile_of, low_of, high_of, along):
    lane = lane_ids()
    tiles = along.shape[1] // 8 - 1
    for c in range(3):
        for t in range(tiles):
            mid = tile_of(c, t)
            low = jnp.where(lane == 0, low_of(c, t), pltpu.roll(mid, 1, 1))
            high = jnp.where(lane == LANES - 1, high_of(c, t), pltpu.roll(mid, LANES - 1, 1))
            for k, v in enumerate(triple(low, mid, high)):
                along[3 * c + k, 8 * t + 8 : 8 * t + 16, :] = v
                if t == tiles - 1:
                    along[3 * c + k, 0:8, :] = v


def rim_shifts(by, t, spot, to_lane):
    n = by // 16
    if t == 2 * n:
        return n, lax.rem(to_lane + LANES - spot, LANES)
    return t % n, lax.rem(to_lane + 2 * LANES - spot - HALF * (t // n), LANES)


def xy_pass(along, ring, slot, emit):
    for t in range(along.shape[1] // 8 - 2):
        rows = slice(8 * t, 8 * t + 8)
        fields = []
        for c in range(3):
            now = {}
            for k, z in enumerate("MDS"):
                three = [along[3 * c + k, 8 * t + 7 + o : 8 * t + 15 + o, :] for o in range(3)]
                if z == "S":
                    now["MS"], now["DS"] = pair(*three)
                else:
                    now["M" + z], now["D" + z], now["S" + z] = triple(*three)
            held = {}
            for k, key in enumerate(YZ):
                f = 8 * c + k
                if emit is not None:
                    held[key] = ring[slot, f, rows, :], ring[1 - slot, f, rows, :], now[key]
                ring[slot, f, rows, :] = now[key]
            fields.append(held)
        if emit is not None:
            emit(t, energy_of(fields))


def inner_kernel(disp, density, flags, trim, yr1, yr2, rims, inner, along0, along1, ring):
    _, bx, by, _ = disp.shape
    odd_y = is_odd("gy")
    tiles = by // 8

    def along_z(x, along):
        def tile_of(c, t):
            if t < tiles:
                return disp[c, x, 8 * t : 8 * t + 8, :]
            return rim_tile(yr1, yr2, c * bx + x, odd_y)

        def rim(side, to_lane):
            def of(c, t):
                tile, turn = rim_shifts(by, t, x, to_lane)
                return pltpu.roll(rims[side * ends_tiles(by) + c * (by // 16 + 1) + tile], turn, 1)

            return of

        z_pass(tile_of, rim(0, 0), rim(1, LANES - 1), along)

    def across(x, along, slot):
        def emit(t, energy):
            rows = slice(8 * t, 8 * t + 8)
            at = jnp.maximum(x - 1, 0)
            coef = cell_coef(density[at, rows, :], flags[at, rows, :], trim[at, rows, :])
            inner[jnp.maximum(x - 2, 0), rows, :] = coef * energy

        xy_pass(along, ring, slot, emit)

    along_z(0, along0)

    def planes_two(k, carry):
        along_z(2 * k + 1, along1)
        across(2 * k, along0, 0)
        along_z(jnp.minimum(2 * k + 2, bx - 1), along0)
        across(2 * k + 1, along1, 1)
        return carry

    lax.fori_loop(0, bx // 2, planes_two, 0)


def outer_kernel(
    disp, density, flags, trim, yr1, yr2, rims, xr1, xr2, inner,
    source, ys1, ys2, packed,
    field, coef, ends, along0, along1, ring,
):
    _, bx, by, _ = disp.shape
    cells, tall = bx + 2 * REACH, by + 8
    planes, coefs, _ = x_rows(by)
    count = WIDE + 2
    odd_x, odd_y = is_odd("gx"), is_odd("gy")
    row = row_ids()
    for side in range(2):
        def pick(at, size, side=side):
            one, two = xr1[at : at + size, :], xr2[at : at + size, :]
            return jnp.where(odd_x, two, one) if side else jnp.where(odd_x, one, two)

        for c in range(3):
            for k in range(WIDE):
                field[side, c, k + 2 * side] = pick((c * WIDE + k) * tall, tall)
            for k in range(2):
                x = bx - 2 + k if side else k
                at = k if side else WIDE + k
                field[side, c, at, 0:by, :] = disp[c, x]
                field[side, c, at, by:tall, :] = rim_tile(yr1, yr2, c * bx + x, odd_y)
        for k in range(REACH):
            coef[side, k + side] = pick(planes + k * by, by)
        x = bx - 1 if side else 0
        coef[side, 0 if side else REACH] = cell_coef(density[x], flags[x], trim[x])
        for j in range(2 * ends_tiles(by)):
            ends[side, j] = pick(coefs + 8 * j, 8)
    for j in range(2 * ends_tiles(by)):
        ends[2, j] = rims[j]

    def one_side(side, carry):
        high_side = side == 1

        def along_z(i, along):
            low_whose = 2 if i >= WIDE else 0
            low_spot = i - WIDE if i >= WIDE else bx - WIDE + i
            high_whose = 2 if i < 2 else 1
            high_spot = bx - 2 + i if i < 2 else i - 2
            whose = jnp.where(high_side, high_whose, low_whose)
            spot = jnp.where(high_side, high_spot, low_spot)

            def rim(z_side, to_lane):
                def of(c, t):
                    tile, turn = rim_shifts(by, t, spot, to_lane)
                    at = z_side * ends_tiles(by) + c * (by // 16 + 1) + tile
                    return pltpu.roll(ends[whose, at], turn, 1)

                return of

            z_pass(
                lambda c, t: field[side, c, i, 8 * t : 8 * t + 8, :],
                rim(0, 0), rim(1, LANES - 1), along,
            )

        alongs = along0, along1
        along_z(0, along0)
        for i in range(count):
            if i + 1 < count:
                along_z(i + 1, alongs[(i + 1) % 2])

            def emit(t, energy, i=i):
                rows = slice(8 * t, 8 * t + 8)
                source[side * (cells - WIDE) + i - 2, rows, :] = coef[side, i - 2, rows, :] * energy

            xy_pass(alongs[i % 2], ring, i % 2, emit if i >= 2 else None)
        return carry

    lax.fori_loop(0, 2, one_side, 0)

    def copy(x, carry):
        source[x + WIDE] = inner[x]
        return carry

    lax.fori_loop(0, bx - 2, copy, 0, unroll=4)

    def rows_out(q, carry):
        top = row < 4
        first, second = source[2 * q, 0:8, :], source[2 * q + 1, 0:8, :]
        low = jnp.where(top, first, half_turn(second))
        first, second = source[2 * q, by - 8 : by, :], source[2 * q + 1, by - 8 : by, :]
        high = jnp.where(top, half_turn(first), second)
        ys1[q] = jnp.where(odd_y, low, high)
        ys2[q] = jnp.where(odd_y, high, low)
        return carry

    lax.fori_loop(0, cells // 2, rows_out, 0, unroll=6)
    pack_columns(source, packed, by)


def pack_columns(source, packed, count):
    cells = source.shape[0]
    row = row_ids()
    for y in range(count):
        tall = jnp.concatenate([source[:, y, :], jnp.zeros((LANES - cells, LANES), F32)], axis=0)
        flat = tall.T
        packed[y] = jnp.where(row < 4, flat[0:8], flat[LANES - 8 : LANES])


def corner_kernel(yr1, yr2, packed, rim, rim_packed, zs1, zs2):
    by = packed.shape[0]
    odd_y, odd_z = is_odd("gy"), is_odd("gz")
    top = row_ids() < 4

    def unpack(q, carry):
        high = jnp.where(odd_y, yr2[q], yr1[q])
        low = jnp.where(odd_y, yr1[q], yr2[q])
        rim[2 * q] = jnp.where(top, high, half_turn(low))
        rim[2 * q + 1] = jnp.where(top, half_turn(high), low)
        return carry

    lax.fori_loop(0, yr1.shape[0], unpack, 0, unroll=6)
    pack_columns(rim, rim_packed, 8)

    def send(m, first, second):
        low = jnp.where(top, first, half_turn(second))
        high = jnp.where(top, half_turn(first), second)
        zs1[m] = jnp.where(odd_z, low, high)
        zs2[m] = jnp.where(odd_z, high, low)

    for m in range(by // 2):
        send(m, packed[2 * m], packed[2 * m + 1])
    for m in range(4):
        send(by // 2 + m, rim_packed[2 * m], rim_packed[2 * m + 1])


def filter_kernel(
    source, rim, packed, rim_packed, zr1, zr2, filtered, partial,
    work0, work1, low_strip, high_strip, strips, ends, joint,
):
    cells, by, _ = source.shape
    bx = cells - 2 * REACH
    tall = by + 8
    odd_z = is_odd("gz")
    lane, row = lane_ids(), row_ids()
    top = row < 4
    first_x, last_x = lax.axis_index("gx") == 0, lax.axis_index("gx") == lax.axis_size("gx") - 1
    first_y, last_y = lax.axis_index("gy") == 0, lax.axis_index("gy") == lax.axis_size("gy") - 1
    first_z, last_z = lax.axis_index("gz") == 0, lax.axis_index("gz") == lax.axis_size("gz") - 1

    for m in range(tall // 2):
        low = jnp.where(odd_z, zr1[m], zr2[m])
        high = jnp.where(odd_z, zr2[m], zr1[m])
        for part in range(2):
            y = 2 * m + part
            own = half_turn(packed[y] if y < by else rim_packed[y - by])
            low_strip[y] = jnp.where(top, half_turn(low) if part else low, own)
            high_strip[y] = jnp.where(top, own, high if part else half_turn(high))

    inside_x = jnp.logical_not(
        jnp.logical_or(
            jnp.logical_and(first_x, lane < REACH),
            jnp.logical_and(last_x, lane >= bx + REACH),
        )
    )
    inside_low = jnp.logical_and(inside_x, jnp.logical_not(jnp.logical_and(first_z, top)))
    inside_high = jnp.logical_and(
        inside_x, jnp.logical_not(jnp.logical_and(last_z, jnp.logical_not(top)))
    )
    for side, strip, edge_row, inside in (
        (0, low_strip, 3, inside_low),
        (1, high_strip, 4, inside_high),
    ):
        strips[0] = POLY[4] * strip[...]
        for k in range(4):
            now, later = k % 2, (k + 1) % 2
            for t in range(tall // 8):
                ends[k, side, 8 * t : 8 * t + 8, :] = strips[now, 8 * t : 8 * t + 8, edge_row, :]
            if k == 3:
                break
            for y in range(tall):
                mid = strips[now, y]
                total = strips[now, (y + 1) % tall] + strips[now, (y - 1) % tall]
                total = total + (pltpu.roll(mid, 1, 1) + pltpu.roll(mid, LANES - 1, 1))
                total = total + (pltpu.roll(mid, 1, 0) + pltpu.roll(mid, 7, 0))
                total = total + POLY[3 - k] * strip[y]
                outside = first_y if y >= by + 4 else last_y
                keep = inside
                if y >= by:
                    keep = jnp.logical_and(inside, jnp.logical_not(outside))
                strips[later, y] = jnp.where(keep, total, 0.0)

    for k in range(4):
        for t in range(tall // 8):
            low = ends[k, 0, 8 * t : 8 * t + 8, :]
            high = pltpu.roll(ends[k, 1, 8 * t : 8 * t + 8, :], LANES - 1, 1)
            even = lax.rem(lane, 2) == 0
            joint[k, 0, 8 * t : 8 * t + 8, :] = jnp.where(even, low, high)
            joint[k, 1, 8 * t : 8 * t + 8, :] = jnp.where(even, high, low)

    def put(ref, x, t, value):
        ref[x, 8 * t + 8 : 8 * t + 16, :] = value
        if t == by // 8:
            ref[x, 0:8, :] = value
        if t == 0:
            ref[x, by + 16 : by + 24, :] = value

    def begin(x, carry):
        for t in range(by // 8):
            put(work0, x, t, POLY[4] * source[x, 8 * t : 8 * t + 8, :])
        put(work0, x, by // 8, POLY[4] * rim[x])
        return carry

    lax.fori_loop(0, cells, begin, 0, unroll=4)
    rim_keep = jnp.logical_not(
        jnp.logical_or(
            jnp.logical_and(last_y, top), jnp.logical_and(first_y, jnp.logical_not(top))
        )
    )
    tiles = by // 8
    total = jnp.zeros((8, LANES), F32)
    for k in range(4):
        now, later = (work0, work1)[k % 2], (work0, work1)[(k + 1) % 2]

        def sweep(x, parity, k=k, now=now, later=later):
            to_first = lax.rem(LANES - x, LANES)
            total = 0.0
            for t in range(tiles + (k < 3)):
                at = 8 * t + 8
                mid = now[x, at : at + 8, :]
                value = now[x - 1, at : at + 8, :] + now[x + 1, at : at + 8, :]
                value = value + (now[x, at - 1 : at + 7, :] + now[x, at + 1 : at + 9, :])
                ends_here = pltpu.roll(joint[k, parity, 8 * t : 8 * t + 8, :], to_first, 1)
                low = jnp.where(lane == 0, ends_here, pltpu.roll(mid, 1, 1))
                high = jnp.where(lane == LANES - 1, ends_here, pltpu.roll(mid, LANES - 1, 1))
                value = value + (low + high)
                own = source[x, 8 * t : 8 * t + 8, :] if t < tiles else rim[x]
                value = value + POLY[3 - k] * own
                if k == 3:
                    filtered[x - REACH, 8 * t : 8 * t + 8, :] = value
                    total = total + jnp.abs(value)
                else:
                    if t == tiles:
                        value = jnp.where(rim_keep, value, 0.0)
                    put(later, x, t, value)
            return total

        first, left = (1, cells - 2) if k < 3 else (REACH, bx)
        group = max(g for g in range(2, 19, 2) if left % g == 0)

        def sweeps(j, total, first=first, group=group, sweep=sweep, k=k):
            for g in range(group):
                more = sweep(first + j * group + g, (first + g) % 2)
                total = total + more if k == 3 else total
            return total

        total = lax.fori_loop(0, left // group, sweeps, total)
        if k < 3:

            @pl.when(first_x)
            def _(later=later):
                later[0:REACH] = jnp.zeros((REACH,) + later.shape[1:], F32)

            @pl.when(last_x)
            def _(later=later):
                later[bx + REACH : cells] = jnp.zeros((REACH,) + later.shape[1:], F32)

    partial[...] = jnp.broadcast_to(jnp.sum(total, axis=0, keepdims=True), partial.shape)


def project_kernel(count, density, filtered, sums, projected):
    scale = jnp.sum(sums[...]) / count + 1e-06
    inverse = jnp.full((8, LANES), 1.0, F32) / scale
    lower = math.tanh(SHARPNESS * THRESHOLD)
    bottom = lower + math.tanh(SHARPNESS * (1.0 - THRESHOLD))

    def one(x, carry):
        for t in range(density.shape[1] // 8):
            rows = slice(8 * t, 8 * t + 8)
            trial = density[x, rows, :] - STEP_SIZE * (filtered[x, rows, :] * inverse + 1.0)
            level = lower + jnp.tanh(SHARPNESS * (trial - THRESHOLD))
            projected[x, rows, :] = level * (1.0 / bottom)
        return carry

    lax.fori_loop(0, density.shape[0], one, 0, unroll=8)


def call(kernel, outs, scratch=(), cost=0):
    return pl.pallas_call(
        kernel,
        out_shape=[jax.ShapeDtypeStruct(s, F32) for s in outs],
        out_specs=[VMEM] * len(outs),
        scratch_shapes=[pltpu.VMEM(s, F32) for s in scratch],
        compiler_params=pltpu.CompilerParams(**PARAMS),
        cost_estimate=pl.CostEstimate(flops=cost, bytes_accessed=cost, transcendentals=0),
    )


def body(displacement, density, cell_flags, trim_level):
    bx, by, bz = density.shape
    assert bz == LANES and bx <= HALF and bx % 2 == 0 and by % 16 == 0
    cells, tall = bx + 2 * REACH, by + 8
    devices = lax.axis_size(AXES)
    odd_y = is_odd("gy")
    given = displacement, density, cell_flags, trim_level

    def y_face(at_low):
        start = jnp.where(at_low, 0, by - 1)
        return lax.dynamic_slice_in_dim(displacement, start, 1, 2).reshape(3 * bx, bz)

    yr1, yr2 = swap(y_face(odd_y), y_face(jnp.logical_not(odd_y)), "gy")
    n = 3 * (by // 16)
    low, high = call(faces_kernel, [(n, 8, LANES)] * 2, cost=6_000_000)(displacement)
    zs1, zs2 = call(ends_kernel, [(n + 1, 8, LANES)] * 2)(low, high, yr1, yr2)
    zr1, zr2 = swap(zs1, zs2, "gz")
    rows = x_rows(by)[2]
    xs1, xs2, rims = call(
        outward_kernel, [(rows, LANES), (rows, LANES), (2 * ends_tiles(by), 8, LANES)]
    )(*given, yr1, yr2, zr1, zr2)
    xr1, xr2 = swap(xs1, xs2, "gx")
    along = (9, by + 16, LANES)
    ring = (2, 24, by, LANES)
    (inner,) = call(
        inner_kernel, [(bx - 2, by, LANES)], [along, along, ring], cost=60_000_000
    )(*given, yr1, yr2, rims)
    source, ys1, ys2, packed = call(
        outer_kernel,
        [(cells, by, LANES), (cells // 2, 8, LANES), (cells // 2, 8, LANES), (by, 8, LANES)],
        [
            (2, 3, WIDE + 2, tall, LANES),
            (2, REACH + 1, by, LANES),
            (3, 2 * ends_tiles(by), 8, LANES),
            along,
            along,
            ring,
        ],
    )(*given, yr1, yr2, rims, xr1, xr2, inner)
    yr1, yr2 = swap(ys1, ys2, "gy")
    rim, rim_packed, zs1, zs2 = call(
        corner_kernel,
        [(cells, 8, LANES), (8, 8, LANES), (tall // 2, 8, LANES), (tall // 2, 8, LANES)],
    )(yr1, yr2, packed)
    zr1, zr2 = swap(zs1, zs2, "gz")
    filtered, partial = call(
        filter_kernel,
        [(bx, by, LANES), (devices, LANES)],
        [
            (cells, by + 24, LANES),
            (cells, by + 24, LANES),
            (tall, 8, LANES),
            (tall, 8, LANES),
            (2, tall, 8, LANES),
            (4, 2, tall, LANES),
            (4, 2, tall, LANES),
        ],
    )(source, rim, packed, rim_packed, zr1, zr2)
    sums = lax.all_to_all(partial, AXES, split_axis=0, concat_axis=0, tiled=True)
    count = float(filtered.size * devices)
    (projected,) = call(functools.partial(project_kernel, count), [(bx, by, LANES)])(
        density, filtered, sums
    )
    return projected, filtered


def solution(mesh):
    return jax.shard_map(
        body,
        mesh=mesh,
        in_specs=(P(None, *AXES), P(*AXES), P(*AXES), P(*AXES)),
        out_specs=(P(*AXES), P(*AXES)),
        check_vma=False,
    )
```

```python
import functools
import math

import jax
import jax.numpy as jnp
import numpy as np
from jax import lax
from jax.experimental import pallas as pl
from jax.experimental.pallas import tpu as pltpu
from jax.sharding import PartitionSpec as P

LAMBDA = 0.3 / 0.52
SHEAR_MODULUS = 1.0 / 2.6
SPREAD_MID = 5.5
SPREAD_HALF = 4.5
STEP_SIZE = 0.3
SHARPNESS = 8.0
THRESHOLD = 0.5

AXES = ("gx", "gy", "gz")
LANES = 128
HALF = 64
REACH = 4
WIDE = REACH + 1

SIGMA = SPREAD_MID / SPREAD_HALF
CHEB = 16.0 * SIGMA**5 - 20.0 * SIGMA**3 + 5.0 * SIGMA
POLY = [
    (16.0 * SIGMA**4 - 20.0 * SIGMA**2 + 5.0) / (SPREAD_HALF * CHEB),
    (16.0 * SIGMA**3 - 20.0 * SIGMA) / 6.0 / (SPREAD_HALF * CHEB),
    (16.0 * SIGMA**2 - 20.0) / 36.0 / (SPREAD_HALF * CHEB),
    16.0 * SIGMA / 216.0 / (SPREAD_HALF * CHEB),
    16.0 / 1296.0 / (SPREAD_HALF * CHEB),
]


def reach_weights():
    power = np.ones((5 + REACH,) * 3)
    total = POLY[0] * power
    for m in range(1, REACH + 1):
        wide = np.pad(np.pad(power, ((0, 1),) * 3, mode="edge"), ((1, 0),) * 3)
        power = sum(
            np.roll(wide, step, dim)[1:-1, 1:-1, 1:-1] for dim in range(3) for step in (1, -1)
        )
        total = total + POLY[m] * power
    return total[:5, :5, :5]


F32 = jnp.float32
VMEM = pl.BlockSpec(memory_space=pltpu.VMEM)
PARAMS = dict(vmem_limit_bytes=20 * 1024 * 1024)


def partners(axis, sizes):
    dim = AXES.index(axis)
    count, near = sizes[dim], 1 if axis == "gz" else 2
    first, second = [], []
    for at in np.ndindex(*sizes):
        for pairs, other in (
            (first, at[dim] ^ 1),
            (second, at[dim] + 1 if at[dim] % 2 else at[dim] - 1),
        ):
            to = list(at)
            if 0 <= other < count:
                to[dim] = other
            elif sizes[near] > 1:
                to[near] ^= 1
            pairs.append(tuple(int(np.ravel_multi_index(v, sizes)) for v in (at, to)))
    return first, second


def swap(first, second, axis):
    sizes = tuple(lax.axis_size(a) for a in AXES)
    near, far_ones = partners(axis, sizes)
    return lax.ppermute(first, AXES, near), lax.ppermute(second, AXES, far_ones)


def at_end(axis):
    at = lax.axis_index(axis)
    return jnp.logical_or(at == 0, at == lax.axis_size(axis) - 1)


def cleared(axis, value):
    return jnp.where(at_end(axis), 0.0, value)


def is_odd(axis):
    return lax.rem(lax.axis_index(axis), 2) == 1


def cell_coef(density, cell_flags, trim_level):
    trimmed = (1.0 + trim_level.astype(F32)) * 0.2
    share = jnp.where(cell_flags == 1, 1.0, jnp.where(cell_flags == 2, trimmed, 0.001))
    return -3.0 * density * density * density * share


def lane_ids():
    return lax.broadcasted_iota(jnp.int32, (8, LANES), 1)


def row_ids():
    return lax.broadcasted_iota(jnp.int32, (8, LANES), 0)


def half_turn(tile):
    return pltpu.roll(tile, 4, 0)


def rim_tile(first, second, index, odd):
    one = jnp.broadcast_to(first[pl.ds(index, 1), :], (8, LANES))
    two = jnp.broadcast_to(second[pl.ds(index, 1), :], (8, LANES))
    at_top = row_ids() == 0
    return jnp.where(jnp.logical_xor(at_top, odd), one, two)


def two_halves(first, second):
    spare = HALF - first.shape[0]
    if spare:
        zero = jnp.zeros((spare, LANES), F32)
        first = jnp.concatenate([first, zero], axis=0)
        second = jnp.concatenate([second, zero], axis=0)
    return jnp.concatenate([first, second], axis=0).T


def sides_kernel(disp, ys1, ys2):
    _, bx, by, _ = disp.shape
    odd_y = is_odd("gy")
    for c in range(3):
        rows = slice(c * bx, c * bx + bx)
        low, high = disp[c, :, 0, :], disp[c, :, by - 1, :]
        ys1[rows, :] = jnp.where(odd_y, low, high)
        ys2[rows, :] = jnp.where(odd_y, high, low)


def faces_kernel(disp, low, high):
    _, _, by, _ = disp.shape
    n = by // 16
    for c in range(3):
        for y in range(by // 2):
            turned = two_halves(disp[c, :, y, :], disp[c, :, y + by // 2, :])
            low[c * n + y // 8, y % 8 : y % 8 + 1, :] = turned[0:1]
            high[c * n + y // 8, y % 8 : y % 8 + 1, :] = turned[LANES - 1 : LANES]


def ends_kernel(low, high, yr1, yr2_raw, zs1, zs2, yr2):
    odd_z = is_odd("gz")
    n, bx = low.shape[0], yr1.shape[0] // 3
    yr2[...] = cleared("gy", yr2_raw[...])
    zs1[0:n] = jnp.where(odd_z, low[...], high[...])
    zs2[0:n] = jnp.where(odd_z, high[...], low[...])
    zs1[n] = jnp.zeros((8, LANES), F32)
    zs2[n] = jnp.zeros((8, LANES), F32)
    for c in range(3):
        rows = slice(c * bx, c * bx + bx)
        turned = two_halves(yr1[rows, :], yr2[rows, :])
        near, far = turned[0:1], turned[LANES - 1 : LANES]
        zs1[n, c : c + 1, :] = jnp.where(odd_z, near, far)
        zs2[n, c : c + 1, :] = jnp.where(odd_z, far, near)


def x_rows(by):
    tall = by + 8
    planes = 3 * WIDE * tall
    coefs = planes + REACH * by
    return planes, coefs, coefs + 2 * 3 * (by // 16 + 1) * 8


def ends_tiles(by):
    return 3 * (by // 16 + 1)


def outward_kernel(disp, coef, yr1, yr2, zr1, zr2, xs1, xs2, rims):
    _, bx, by, _ = disp.shape
    tall, n = by + 8, by // 16
    odd_x, odd_y, odd_z = is_odd("gx"), is_odd("gy"), is_odd("gz")
    top_row, left = row_ids() == 0, lane_ids() < HALF
    for side in range(2):
        def pick(*at, side=side):
            one, two = zr1[at], cleared("gz", zr2[at])
            return jnp.where(odd_z, two, one) if side else jnp.where(odd_z, one, two)

        for c in range(3):
            base = side * ends_tiles(by) + c * (n + 1)
            for t in range(n):
                rims[base + t] = pick(c * n + t)
            both = jnp.broadcast_to(pick(3 * n, slice(c, c + 1), slice(None)), (8, LANES))
            other = pltpu.roll(both, HALF, 1)
            rims[base + n] = jnp.where(jnp.logical_xor(top_row, odd_y), both, other)
    planes, coefs, _ = x_rows(by)
    for out, at_low in ((xs1, odd_x), (xs2, jnp.logical_not(odd_x))):
        start = jnp.where(at_low, 0, bx - WIDE)
        for c in range(3):
            for k in range(WIDE):
                at = (c * WIDE + k) * tall
                out[at : at + by, :] = disp[c, start + k]
                out[at + by : at + tall, :] = rim_tile(yr1, yr2, c * bx + start + k, odd_y)
        start = jnp.where(at_low, 0, bx - REACH)
        for k in range(REACH):
            out[planes + k * by : planes + (k + 1) * by, :] = coef[start + k]
        for j in range(2 * ends_tiles(by)):
            out[coefs + 8 * j : coefs + 8 * j + 8, :] = rims[j]


def triple(a, b, c):
    ends = a + c
    curve = ends - 2.0 * b
    return 4.0 * b + (2.0 / 3.0) * curve, c - a, curve


def pair(a, b, c):
    return (2.0 / 3.0) * (a + c) + (8.0 / 3.0) * b, c - a


FIELDS = (
    [(0, key) for key in ("MM", "MD", "MS", "DM", "DD", "DS", "SM", "SD")]
    + [(1, key) for key in ("MM", "MD", "DM", "DD", "SM", "SD")]
    + [(2, key) for key in ("MM", "MD", "DM", "DD", "MS", "DS")]
    + [(3, key) for key in ("00", "01", "10", "11")]
)
ALL_THREE = {(0, "MD"), (0, "DM"), (0, "DD"), (1, "DM"), (1, "DD"), (2, "MD"), (2, "DD")}
NO_VALUE = {(0, "MM"), (1, "MM"), (1, "MD"), (2, "MM"), (2, "DM")}


def energy_of(fields):
    grads = {}
    for name, planes in fields.items():
        if name in NO_VALUE:
            a, b, n = planes
            grads[name + ("D",)], grads[name + ("S",)] = n - a, (a + n) - 2.0 * b
        elif name in ALL_THREE:
            three = triple(*planes)
            grads.update({name + (x,): v for x, v in zip("MDS", three)})
        else:
            grads.update({name + (x,): v for x, v in zip("MD", pair(*planes))})
    names = "MD", "DS"

    def part(c, e, p):
        ops = [names[1 if d == e else 0][p[d]] for d in range(3)]
        return grads[(c, ops[1] + ops[2], ops[0])]

    traces = mixed = shears = None
    for order in (3, 2, 1, 0):
        if traces is not None:
            traces, mixed, shears = (v * (1.0 / 3.0) for v in (traces, mixed, shears))
        for bits in range(8):
            p = (bits >> 2) & 1, (bits >> 1) & 1, bits & 1
            if sum(p) != order:
                continue
            xx, yy, zz = (part(c, c, p) for c in range(3))
            xy = part(0, 1, p) + part(1, 0, p)
            xz = part(0, 2, p) + part(2, 0, p)
            yz = grads[(3, "%d%d" % p[1:], "MD"[p[0]])]
            both = xx + yy
            trace = both + zz
            trace = trace * trace
            mix = xx * yy + both * zz
            shear = xy * xy + xz * xz + yz * yz
            if traces is None:
                traces, mixed, shears = trace, mix, shear
            else:
                traces, mixed, shears = traces + trace, mixed + mix, shears + shear
    scale = 1.0 / 1024.0
    return (
        ((LAMBDA + 2.0 * SHEAR_MODULUS) * scale) * traces
        - (4.0 * SHEAR_MODULUS * scale) * mixed
        + (SHEAR_MODULUS * scale) * shears
    )


def z_pass(tile_of, low_of, high_of, along):
    lane = lane_ids()
    tiles = along.shape[1] // 8 - 1
    for c in range(3):
        for t in range(tiles):
            mid = tile_of(c, t)
            low = jnp.where(lane == 0, low_of(c, t), pltpu.roll(mid, 1, 1))
            high = jnp.where(lane == LANES - 1, high_of(c, t), pltpu.roll(mid, LANES - 1, 1))
            for k, v in enumerate(triple(low, mid, high)):
                along[3 * c + k, 8 * t + 8 : 8 * t + 16, :] = v
                if t == tiles - 1:
                    along[3 * c + k, 0:8, :] = v


def rim_shifts(by, t, spot, to_lane):
    n = by // 16
    if t == 2 * n:
        return n, lax.rem(to_lane + LANES - spot, LANES)
    return t % n, lax.rem(to_lane + 2 * LANES - spot - HALF * (t // n), LANES)


def xy_pass(along, ring, slot, emit):
    for t in range(along.shape[1] // 8 - 2):
        rows = slice(8 * t, 8 * t + 8)
        now = {}
        for c in range(3):
            for k, z in enumerate("MDS"):
                three = [along[3 * c + k, 8 * t + 7 + o : 8 * t + 15 + o, :] for o in range(3)]
                values = pair(*three) if z == "S" else triple(*three)
                now.update({(c, y + z): v for y, v in zip("MDS", values)})
        now[(3, "00")] = now[(2, "DM")] + now[(1, "MD")]
        now[(3, "01")] = now[(2, "DD")] + now[(1, "MS")]
        now[(3, "10")] = now[(2, "SM")] + now[(1, "DD")]
        now[(3, "11")] = now[(2, "SD")] + now[(1, "DS")]
        fields = {}
        for f, name in enumerate(FIELDS):
            if emit is not None:
                fields[name] = ring[slot, f, rows, :], ring[1 - slot, f, rows, :], now[name]
            ring[slot, f, rows, :] = now[name]
        if emit is not None:
            emit(t, energy_of(fields))


def far(axis, index, size):
    at = lax.axis_index(axis) * size + index
    return jnp.minimum(jnp.minimum(at, lax.axis_size(axis) * size - 1 - at), REACH)


def fill_weights(weights):
    table = reach_weights()
    by = weights.shape[1]
    far_z = far("gz", lane_ids(), LANES)
    for d in range(REACH + 1):
        for t in range(by // 8):
            far_y = far("gy", row_ids() + 8 * t, by)
            value = None
            for j in range(REACH, -1, -1):
                line = jnp.full((8, LANES), table[d, j, REACH], F32)
                for k in range(REACH):
                    line = jnp.where(far_z == k, F32(table[d, j, k]), line)
                value = line if value is None else jnp.where(far_y == j, line, value)
            weights[d, 8 * t : 8 * t + 8, :] = value


def inner_kernel(disp, coef, yr1, yr2, rims, inner, partial, weights, along0, along1, ring):
    _, bx, by, _ = disp.shape
    odd_y = is_odd("gy")
    tiles = by // 8
    fill_weights(weights)

    def along_z(x, along):
        def tile_of(c, t):
            if t < tiles:
                return disp[c, x, 8 * t : 8 * t + 8, :]
            return rim_tile(yr1, yr2, c * bx + x, odd_y)

        def rim(side, to_lane):
            def of(c, t):
                tile, turn = rim_shifts(by, t, x, to_lane)
                return pltpu.roll(rims[side * ends_tiles(by) + c * (by // 16 + 1) + tile], turn, 1)

            return of

        z_pass(tile_of, rim(0, 0), rim(1, LANES - 1), along)

    def across(x, along, slot, total):
        totals = [total]

        def emit(t, energy):
            rows = slice(8 * t, 8 * t + 8)
            value = coef[x - 1, rows, :] * energy
            inner[x - 2, rows, :] = value
            totals.append(totals[-1] + weights[far("gx", x - 1, bx), rows, :] * value)

        xy_pass(along, ring, slot, emit if total is not None else None)
        return totals[-1]

    along_z(0, along0)
    along_z(1, along1)
    across(0, along0, 0, None)
    along_z(2, along0)
    across(1, along1, 1, None)

    def planes_two(k, total):
        along_z(2 * k + 1, along1)
        total = across(2 * k, along0, 0, total)
        along_z(jnp.minimum(2 * k + 2, bx - 1), along0)
        return across(2 * k + 1, along1, 1, total)

    partial[...] = lax.fori_loop(1, bx // 2, planes_two, jnp.zeros((8, LANES), F32))


def outer_kernel(
    disp, coef, yr1, yr2, rims, xr1, xr2, inner, partial, weights,
    source, ys1, ys2, total,
    field, rim_coef, ends, along0, along1, ring,
):
    _, bx, by, _ = disp.shape
    cells, tall = bx + 2 * REACH, by + 8
    planes, coefs, _ = x_rows(by)
    count = WIDE + 2
    odd_x, odd_y = is_odd("gx"), is_odd("gy")
    row = row_ids()
    for side in range(2):
        def pick(at, size, side=side):
            one, two = xr1[at : at + size, :], cleared("gx", xr2[at : at + size, :])
            return jnp.where(odd_x, two, one) if side else jnp.where(odd_x, one, two)

        for c in range(3):
            for k in range(WIDE):
                field[side, c, k + 2 * side] = pick((c * WIDE + k) * tall, tall)
            for k in range(2):
                x = bx - 2 + k if side else k
                at = k if side else WIDE + k
                field[side, c, at, 0:by, :] = disp[c, x]
                field[side, c, at, by:tall, :] = rim_tile(yr1, yr2, c * bx + x, odd_y)
        for k in range(REACH):
            rim_coef[side, k + side] = pick(planes + k * by, by)
        rim_coef[side, 0 if side else REACH] = coef[bx - 1 if side else 0]
        for j in range(2 * ends_tiles(by)):
            ends[side, j] = pick(coefs + 8 * j, 8)
    for j in range(2 * ends_tiles(by)):
        ends[2, j] = rims[j]
    total[...] = partial[...]

    def one_side(side, carry):
        high_side = side == 1

        def along_z(i, along):
            low_whose = 2 if i >= WIDE else 0
            low_spot = i - WIDE if i >= WIDE else bx - WIDE + i
            high_whose = 2 if i < 2 else 1
            high_spot = bx - 2 + i if i < 2 else i - 2
            whose = jnp.where(high_side, high_whose, low_whose)
            spot = jnp.where(high_side, high_spot, low_spot)

            def rim(z_side, to_lane):
                def of(c, t):
                    tile, turn = rim_shifts(by, t, spot, to_lane)
                    at = z_side * ends_tiles(by) + c * (by // 16 + 1) + tile
                    return pltpu.roll(ends[whose, at], turn, 1)

                return of

            z_pass(
                lambda c, t: field[side, c, i, 8 * t : 8 * t + 8, :],
                rim(0, 0), rim(1, LANES - 1), along,
            )

        alongs = along0, along1
        along_z(0, along0)
        for i in range(count):
            if i + 1 < count:
                along_z(i + 1, alongs[(i + 1) % 2])

            def emit(t, energy, i=i):
                rows = slice(8 * t, 8 * t + 8)
                value = rim_coef[side, i - 2, rows, :] * energy
                source[side * (cells - WIDE) + i - 2, rows, :] = value
                if i in (2, count - 1):
                    own = high_side if i == 2 else jnp.logical_not(high_side)
                    weight = weights[far("gx", bx - 1 if i == 2 else 0, bx), rows, :]
                    total[...] += jnp.where(own, weight * value, 0.0)

            xy_pass(alongs[i % 2], ring, i % 2, emit if i >= 2 else None)
        return carry

    lax.fori_loop(0, 2, one_side, 0)
    def copy(x, carry):
        source[x + WIDE] = inner[x]
        return carry

    lax.fori_loop(0, bx - 2, copy, 0, unroll=4)

    def rows_out(q, carry):
        top = row < 4
        first, second = source[2 * q, 0:8, :], source[2 * q + 1, 0:8, :]
        low = jnp.where(top, first, half_turn(second))
        first, second = source[2 * q, by - 8 : by, :], source[2 * q + 1, by - 8 : by, :]
        high = jnp.where(top, half_turn(first), second)
        ys1[q] = jnp.where(odd_y, low, high)
        ys2[q] = jnp.where(odd_y, high, low)
        return carry

    lax.fori_loop(0, cells // 2, rows_out, 0, unroll=6)


def pack_columns(source, packed, count):
    cells = source.shape[0]
    row = row_ids()
    for y in range(count):
        tall = jnp.concatenate([source[:, y, :], jnp.zeros((LANES - cells, LANES), F32)], axis=0)
        flat = tall.T
        packed[y] = jnp.where(row < 4, flat[0:8], flat[LANES - 8 : LANES])


def pack_kernel(source, total, packed, sums):
    pack_columns(source, packed, source.shape[1])
    sums[...] = jnp.broadcast_to(jnp.sum(total[...], axis=0, keepdims=True), sums.shape)


def corner_kernel(yr1, yr2, packed, rim, rim_packed, zs1, zs2):
    by = packed.shape[0]
    odd_y, odd_z = is_odd("gy"), is_odd("gz")
    top = row_ids() < 4

    def unpack(q, carry):
        one, two = yr1[q], cleared("gy", yr2[q])
        high = jnp.where(odd_y, two, one)
        low = jnp.where(odd_y, one, two)
        rim[2 * q] = jnp.where(top, high, half_turn(low))
        rim[2 * q + 1] = jnp.where(top, half_turn(high), low)
        return carry

    lax.fori_loop(0, yr1.shape[0], unpack, 0, unroll=6)
    pack_columns(rim, rim_packed, 8)

    def send(m, first, second):
        low = jnp.where(top, first, half_turn(second))
        high = jnp.where(top, half_turn(first), second)
        zs1[m] = jnp.where(odd_z, low, high)
        zs2[m] = jnp.where(odd_z, high, low)

    for m in range(by // 2):
        send(m, packed[2 * m], packed[2 * m + 1])
    for m in range(4):
        send(by // 2 + m, rim_packed[2 * m], rim_packed[2 * m + 1])


def filter_kernel(
    count, source, rim, packed, rim_packed, zr1, zr2, density, sums, projected_out, filtered_out,
    work0, work1, low_strip, high_strip, strips, ends, joint, projected, filtered, sems,
):
    cells, by, _ = source.shape
    bx = cells - 2 * REACH
    tall = by + 8
    odd_z = is_odd("gz")
    lane, row = lane_ids(), row_ids()
    top = row < 4
    first_x, last_x = lax.axis_index("gx") == 0, lax.axis_index("gx") == lax.axis_size("gx") - 1
    first_y, last_y = lax.axis_index("gy") == 0, lax.axis_index("gy") == lax.axis_size("gy") - 1
    first_z, last_z = lax.axis_index("gz") == 0, lax.axis_index("gz") == lax.axis_size("gz") - 1

    for m in range(tall // 2):
        one, two = zr1[m], cleared("gz", zr2[m])
        low = jnp.where(odd_z, one, two)
        high = jnp.where(odd_z, two, one)
        for part in range(2):
            y = 2 * m + part
            own = half_turn(packed[y] if y < by else rim_packed[y - by])
            low_strip[y] = jnp.where(top, half_turn(low) if part else low, own)
            high_strip[y] = jnp.where(top, own, high if part else half_turn(high))

    inside_x = jnp.logical_not(
        jnp.logical_or(
            jnp.logical_and(first_x, lane < REACH),
            jnp.logical_and(last_x, lane >= bx + REACH),
        )
    )
    inside_low = jnp.logical_and(inside_x, jnp.logical_not(jnp.logical_and(first_z, top)))
    inside_high = jnp.logical_and(
        inside_x, jnp.logical_not(jnp.logical_and(last_z, jnp.logical_not(top)))
    )
    for side, strip, edge_row, inside in (
        (0, low_strip, 3, inside_low),
        (1, high_strip, 4, inside_high),
    ):
        strips[0] = POLY[4] * strip[...]
        for k in range(4):
            now, later = k % 2, (k + 1) % 2
            for t in range(tall // 8):
                ends[k, side, 8 * t : 8 * t + 8, :] = strips[now, 8 * t : 8 * t + 8, edge_row, :]
            if k == 3:
                break
            for y in range(tall):
                mid = strips[now, y]
                total = strips[now, (y + 1) % tall] + strips[now, (y - 1) % tall]
                total = total + (pltpu.roll(mid, 1, 1) + pltpu.roll(mid, LANES - 1, 1))
                total = total + (pltpu.roll(mid, 1, 0) + pltpu.roll(mid, 7, 0))
                total = total + POLY[3 - k] * strip[y]
                outside = first_y if y >= by + 4 else last_y
                keep = inside
                if y >= by:
                    keep = jnp.logical_and(inside, jnp.logical_not(outside))
                strips[later, y] = jnp.where(keep, total, 0.0)

    for k in range(4):
        for t in range(tall // 8):
            low = ends[k, 0, 8 * t : 8 * t + 8, :]
            high = pltpu.roll(ends[k, 1, 8 * t : 8 * t + 8, :], LANES - 1, 1)
            even = lax.rem(lane, 2) == 0
            joint[k, 0, 8 * t : 8 * t + 8, :] = jnp.where(even, low, high)
            joint[k, 1, 8 * t : 8 * t + 8, :] = jnp.where(even, high, low)

    def put(ref, x, t, value):
        ref[x, 8 * t + 8 : 8 * t + 16, :] = value
        if t == by // 8:
            ref[x, 0:8, :] = value
        if t == 0:
            ref[x, by + 16 : by + 24, :] = value

    def begin(x, carry):
        for t in range(by // 8):
            put(work0, x, t, POLY[4] * source[x, 8 * t : 8 * t + 8, :])
        put(work0, x, by // 8, POLY[4] * rim[x])
        return carry

    lax.fori_loop(0, cells, begin, 0, unroll=4)
    rim_keep = jnp.logical_not(
        jnp.logical_or(
            jnp.logical_and(last_y, top), jnp.logical_and(first_y, jnp.logical_not(top))
        )
    )
    tiles = by // 8
    scale = jnp.full((8, LANES), -jnp.sum(sums[...]) / count, F32) + 1e-06
    inverse = 1.0 / scale
    lower = math.tanh(SHARPNESS * THRESHOLD)
    bottom = 1.0 / (lower + math.tanh(SHARPNESS * (1.0 - THRESHOLD)))
    for k in range(4):
        now, later = (work0, work1)[k % 2], (work0, work1)[(k + 1) % 2]

        def sweep(x, parity, k=k, now=now, later=later):
            to_first = lax.rem(LANES - x, LANES)
            for t in range(tiles + (k < 3)):
                at = 8 * t + 8
                mid = now[x, at : at + 8, :]
                value = now[x - 1, at : at + 8, :] + now[x + 1, at : at + 8, :]
                value = value + (now[x, at - 1 : at + 7, :] + now[x, at + 1 : at + 9, :])
                ends_here = pltpu.roll(joint[k, parity, 8 * t : 8 * t + 8, :], to_first, 1)
                low = jnp.where(lane == 0, ends_here, pltpu.roll(mid, 1, 1))
                high = jnp.where(lane == LANES - 1, ends_here, pltpu.roll(mid, LANES - 1, 1))
                value = value + (low + high)
                own = source[x, 8 * t : 8 * t + 8, :] if t < tiles else rim[x]
                value = value + POLY[3 - k] * own
                if k == 3:
                    rows = slice(8 * t, 8 * t + 8)
                    filtered[x - REACH, rows, :] = value
                    trial = density[x - REACH, rows, :] - STEP_SIZE * (value * inverse + 1.0)
                    level = lower + jnp.tanh(SHARPNESS * (trial - THRESHOLD))
                    projected[x - REACH, rows, :] = level * bottom
                else:
                    if t == tiles:
                        value = jnp.where(rim_keep, value, 0.0)
                    put(later, x, t, value)

        first, left = (1, cells - 2) if k < 3 else (REACH, bx)
        group = max(g for g in range(2, 19, 2) if left % g == 0)

        def sweeps(j, carry, first=first, group=group, sweep=sweep):
            for g in range(group):
                sweep(first + j * group + g, (first + g) % 2)
            return carry

        def leave(j, group=group):
            at = pl.ds(j * group, group)
            return [
                pltpu.make_async_copy(here.at[at], there.at[at], sems.at[i, j])
                for i, (here, there) in enumerate(
                    ((projected, projected_out), (filtered, filtered_out))
                )
            ]

        if k < 3:
            lax.fori_loop(0, left // group, sweeps, 0)
        else:
            for j in range(left // group):
                sweeps(j, 0)
                for copy in leave(j):
                    copy.start()
            for j in range(left // group):
                for copy in leave(j):
                    copy.wait()
        if k < 3:

            @pl.when(first_x)
            def _(later=later):
                later[0:REACH] = jnp.zeros((REACH,) + later.shape[1:], F32)

            @pl.when(last_x)
            def _(later=later):
                later[bx + REACH : cells] = jnp.zeros((REACH,) + later.shape[1:], F32)


def call(kernel, outs, scratch=(), cost=0, out_place=VMEM):
    return pl.pallas_call(
        kernel,
        out_shape=[jax.ShapeDtypeStruct(s, F32) for s in outs],
        out_specs=[out_place] * len(outs),
        scratch_shapes=[pltpu.VMEM(s, F32) if isinstance(s, tuple) else s for s in scratch],
        compiler_params=pltpu.CompilerParams(**PARAMS),
        cost_estimate=pl.CostEstimate(flops=cost, bytes_accessed=cost, transcendentals=0),
    )


def body(displacement, density, cell_flags, trim_level):
    bx, by, bz = density.shape
    assert bz == LANES and bx <= HALF and bx % 2 == 0 and by % 16 == 0
    cells, tall = bx + 2 * REACH, by + 8
    devices = lax.axis_size(AXES)
    ys1, ys2 = call(sides_kernel, [(3 * bx, LANES)] * 2)(displacement)
    yr1, yr2 = swap(ys1, ys2, "gy")
    n = 3 * (by // 16)
    low, high = call(faces_kernel, [(n, 8, LANES)] * 2, cost=6_000_000)(displacement)
    zs1, zs2, yr2 = call(ends_kernel, [(n + 1, 8, LANES)] * 2 + [(3 * bx, LANES)])(
        low, high, yr1, yr2
    )
    zr1, zr2 = swap(zs1, zs2, "gz")
    flags_here, zs1 = lax.optimization_barrier((cell_flags, zs1))
    coef = cell_coef(density, flags_here, trim_level)
    brick = (bx, by, LANES)
    rows = x_rows(by)[2]
    xs1, xs2, rims = call(
        outward_kernel, [(rows, LANES), (rows, LANES), (2 * ends_tiles(by), 8, LANES)]
    )(displacement, coef, yr1, yr2, zr1, zr2)
    xr1, xr2 = swap(xs1, xs2, "gx")
    along = (9, by + 16, LANES)
    ring = (2, 24, by, LANES)
    inner, partial, weights = call(
        inner_kernel,
        [(bx - 2, by, LANES), (8, LANES), (REACH + 1, by, LANES)],
        [along, along, ring],
        cost=60_000_000,
    )(displacement, coef, yr1, yr2, rims)
    source, ys1, ys2, total = call(
        outer_kernel,
        [
            (cells, by, LANES),
            (cells // 2, 8, LANES),
            (cells // 2, 8, LANES),
            (8, LANES),
        ],
        [
            (2, 3, WIDE + 2, tall, LANES),
            (2, REACH + 1, by, LANES),
            (3, 2 * ends_tiles(by), 8, LANES),
            along,
            along,
            ring,
        ],
    )(displacement, coef, yr1, yr2, rims, xr1, xr2, inner, partial, weights)
    yr1, yr2 = swap(ys1, ys2, "gy")
    packed, sums = call(pack_kernel, [(by, 8, LANES), (devices, LANES)])(source, total)
    sums = lax.all_to_all(sums, AXES, split_axis=0, concat_axis=0, tiled=True)
    rim, rim_packed, zs1, zs2 = call(
        corner_kernel,
        [(cells, 8, LANES), (8, 8, LANES), (tall // 2, 8, LANES), (tall // 2, 8, LANES)],
    )(yr1, yr2, packed)
    zr1, zr2 = swap(zs1, zs2, "gz")
    return call(
        functools.partial(filter_kernel, float(bx * by * bz * devices)),
        [brick, brick],
        [
            (cells, by + 24, LANES),
            (cells, by + 24, LANES),
            (tall, 8, LANES),
            (tall, 8, LANES),
            (2, tall, 8, LANES),
            (4, 2, tall, LANES),
            (4, 2, tall, LANES),
            brick,
            brick,
            pltpu.SemaphoreType.DMA((2, bx)),
        ],
        out_place=pl.BlockSpec(memory_space=pl.ANY),
    )(source, rim, packed, rim_packed, zr1, zr2, density, sums)


def solution(mesh):
    return jax.shard_map(
        body,
        mesh=mesh,
        in_specs=(P(None, *AXES), P(*AXES), P(*AXES), P(*AXES)),
        out_specs=(P(*AXES), P(*AXES)),
        check_vma=False,
    )
```

```python
import functools
import math

import jax
import jax.numpy as jnp
import numpy as np
from jax import lax
from jax.experimental import pallas as pl
from jax.experimental.pallas import tpu as pltpu
from jax.sharding import PartitionSpec as P

LAMBDA = 0.3 / 0.52
SHEAR_MODULUS = 1.0 / 2.6
SPREAD_MID = 5.5
SPREAD_HALF = 4.5
STEP_SIZE = 0.3
SHARPNESS = 8.0
THRESHOLD = 0.5

AXES = ("gx", "gy", "gz")
LANES = 128
HALF = 64
REACH = 4
WIDE = REACH + 1

SIGMA = SPREAD_MID / SPREAD_HALF
CHEB = 16.0 * SIGMA**5 - 20.0 * SIGMA**3 + 5.0 * SIGMA
POLY = [
    (16.0 * SIGMA**4 - 20.0 * SIGMA**2 + 5.0) / (SPREAD_HALF * CHEB),
    (16.0 * SIGMA**3 - 20.0 * SIGMA) / 6.0 / (SPREAD_HALF * CHEB),
    (16.0 * SIGMA**2 - 20.0) / 36.0 / (SPREAD_HALF * CHEB),
    16.0 * SIGMA / 216.0 / (SPREAD_HALF * CHEB),
    16.0 / 1296.0 / (SPREAD_HALF * CHEB),
]


def reach_weights():
    power = np.ones((5 + REACH,) * 3)
    total = POLY[0] * power
    for m in range(1, REACH + 1):
        wide = np.pad(np.pad(power, ((0, 1),) * 3, mode="edge"), ((1, 0),) * 3)
        power = sum(
            np.roll(wide, step, dim)[1:-1, 1:-1, 1:-1] for dim in range(3) for step in (1, -1)
        )
        total = total + POLY[m] * power
    return total[:5, :5, :5]


F32 = jnp.float32
VMEM = pl.BlockSpec(memory_space=pltpu.VMEM)
ANYWHERE = pl.BlockSpec(memory_space=pl.ANY)
PARAMS = dict(vmem_limit_bytes=20 * 1024 * 1024)


def partners(axis, sizes):
    dim = AXES.index(axis)
    count, near = sizes[dim], 1 if axis == "gz" else 2
    first, second = [], []
    for at in np.ndindex(*sizes):
        for pairs, other in (
            (first, at[dim] ^ 1),
            (second, at[dim] + 1 if at[dim] % 2 else at[dim] - 1),
        ):
            to = list(at)
            if 0 <= other < count:
                to[dim] = other
            elif sizes[near] > 1:
                to[near] ^= 1
            pairs.append(tuple(int(np.ravel_multi_index(v, sizes)) for v in (at, to)))
    return first, second


def swap(first, second, axis):
    sizes = tuple(lax.axis_size(a) for a in AXES)
    near, far_ones = partners(axis, sizes)
    return lax.ppermute(first, AXES, near), lax.ppermute(second, AXES, far_ones)


def at_end(axis):
    at = lax.axis_index(axis)
    return jnp.logical_or(at == 0, at == lax.axis_size(axis) - 1)


def cleared(axis, value):
    return jnp.where(at_end(axis), 0.0, value)


def is_odd(axis):
    return lax.rem(lax.axis_index(axis), 2) == 1


def cell_coef(density, cell_flags, trim_level):
    trimmed = (1.0 + trim_level.astype(F32)) * 0.2
    share = jnp.where(cell_flags == 1, 1.0, jnp.where(cell_flags == 2, trimmed, 0.001))
    return -3.0 * density * density * density * share


def lane_ids():
    return lax.broadcasted_iota(jnp.int32, (8, LANES), 1)


def row_ids():
    return lax.broadcasted_iota(jnp.int32, (8, LANES), 0)


def half_turn(tile):
    return pltpu.roll(tile, 4, 0)


def rim_tile(first, second, index, odd):
    one = jnp.broadcast_to(first[pl.ds(index, 1), :], (8, LANES))
    two = jnp.broadcast_to(second[pl.ds(index, 1), :], (8, LANES))
    at_top = row_ids() == 0
    return jnp.where(jnp.logical_xor(at_top, odd), one, two)


def two_halves(first, second):
    spare = HALF - first.shape[0]
    if spare:
        zero = jnp.zeros((spare, LANES), F32)
        first = jnp.concatenate([first, zero], axis=0)
        second = jnp.concatenate([second, zero], axis=0)
    return jnp.concatenate([first, second], axis=0).T


def sides_kernel(disp, ys1, ys2):
    _, bx, by, _ = disp.shape
    odd_y = is_odd("gy")
    for c in range(3):
        rows = slice(c * bx, c * bx + bx)
        low, high = disp[c, :, 0, :], disp[c, :, by - 1, :]
        ys1[rows, :] = jnp.where(odd_y, low, high)
        ys2[rows, :] = jnp.where(odd_y, high, low)


def faces_kernel(disp, low, high):
    _, _, by, _ = disp.shape
    n = by // 16
    for c in range(3):
        for y in range(by // 2):
            turned = two_halves(disp[c, :, y, :], disp[c, :, y + by // 2, :])
            low[c * n + y // 8, y % 8 : y % 8 + 1, :] = turned[0:1]
            high[c * n + y // 8, y % 8 : y % 8 + 1, :] = turned[LANES - 1 : LANES]


def ends_kernel(low, high, yr1, yr2_raw, zs1, zs2, yr2):
    odd_z = is_odd("gz")
    n, bx = low.shape[0], yr1.shape[0] // 3
    yr2[...] = cleared("gy", yr2_raw[...])
    zs1[0:n] = jnp.where(odd_z, low[...], high[...])
    zs2[0:n] = jnp.where(odd_z, high[...], low[...])
    zs1[n] = jnp.zeros((8, LANES), F32)
    zs2[n] = jnp.zeros((8, LANES), F32)
    for c in range(3):
        rows = slice(c * bx, c * bx + bx)
        turned = two_halves(yr1[rows, :], yr2[rows, :])
        near, far = turned[0:1], turned[LANES - 1 : LANES]
        zs1[n, c : c + 1, :] = jnp.where(odd_z, near, far)
        zs2[n, c : c + 1, :] = jnp.where(odd_z, far, near)


def x_rows(by):
    tall = by + 8
    planes = 3 * WIDE * tall
    coefs = planes + REACH * by
    return planes, coefs, coefs + 2 * 3 * (by // 16 + 1) * 8


def ends_tiles(by):
    return 3 * (by // 16 + 1)


def outward_kernel(disp, coef, yr1, yr2, zr1, zr2, xs1, xs2, rims):
    _, bx, by, _ = disp.shape
    tall, n = by + 8, by // 16
    odd_x, odd_y, odd_z = is_odd("gx"), is_odd("gy"), is_odd("gz")
    top_row, left = row_ids() == 0, lane_ids() < HALF
    for side in range(2):
        def pick(*at, side=side):
            one, two = zr1[at], cleared("gz", zr2[at])
            return jnp.where(odd_z, two, one) if side else jnp.where(odd_z, one, two)

        for c in range(3):
            base = side * ends_tiles(by) + c * (n + 1)
            for t in range(n):
                rims[base + t] = pick(c * n + t)
            both = jnp.broadcast_to(pick(3 * n, slice(c, c + 1), slice(None)), (8, LANES))
            other = pltpu.roll(both, HALF, 1)
            rims[base + n] = jnp.where(jnp.logical_xor(top_row, odd_y), both, other)
    planes, coefs, _ = x_rows(by)
    for out, at_low in ((xs1, odd_x), (xs2, jnp.logical_not(odd_x))):
        start = jnp.where(at_low, 0, bx - WIDE)
        for c in range(3):
            for k in range(WIDE):
                at = (c * WIDE + k) * tall
                out[at : at + by, :] = disp[c, start + k]
                out[at + by : at + tall, :] = rim_tile(yr1, yr2, c * bx + start + k, odd_y)
        start = jnp.where(at_low, 0, bx - REACH)
        for k in range(REACH):
            out[planes + k * by : planes + (k + 1) * by, :] = coef[start + k]
        for j in range(2 * ends_tiles(by)):
            out[coefs + 8 * j : coefs + 8 * j + 8, :] = rims[j]


def triple(a, b, c):
    ends = a + c
    curve = ends - 2.0 * b
    return 4.0 * b + (2.0 / 3.0) * curve, c - a, curve


def pair(a, b, c):
    return (2.0 / 3.0) * (a + c) + (8.0 / 3.0) * b, c - a


FIELDS = (
    [(0, key) for key in ("MM", "MD", "MS", "DM", "DD", "DS", "SM", "SD")]
    + [(1, key) for key in ("MM", "MD", "DM", "DD", "SM", "SD")]
    + [(2, key) for key in ("MM", "MD", "DM", "DD", "MS", "DS")]
    + [(3, key) for key in ("00", "01", "10", "11")]
)
ALL_THREE = {(0, "MD"), (0, "DM"), (0, "DD"), (1, "DM"), (1, "DD"), (2, "MD"), (2, "DD")}
NO_VALUE = {(0, "MM"), (1, "MM"), (1, "MD"), (2, "MM"), (2, "DM")}


def energy_of(fields):
    grads = {}
    for name, planes in fields.items():
        if name in NO_VALUE or name in ALL_THREE:
            mid, before, after = planes
            curve = after - before
            grads[name + ("D",)], grads[name + ("S",)] = before + after, curve
            if name in ALL_THREE:
                grads[name + ("M",)] = 4.0 * mid + (2.0 / 3.0) * curve
        else:
            grads.update({name + (x,): v for x, v in zip("MD", pair(*planes))})
    names = "MD", "DS"

    def part(c, e, p):
        ops = [names[1 if d == e else 0][p[d]] for d in range(3)]
        return grads[(c, ops[1] + ops[2], ops[0])]

    traces = mixed = shears = None
    for order in (3, 2, 1, 0):
        if traces is not None:
            traces, mixed, shears = (v * (1.0 / 3.0) for v in (traces, mixed, shears))
        for bits in range(8):
            p = (bits >> 2) & 1, (bits >> 1) & 1, bits & 1
            if sum(p) != order:
                continue
            xx, yy, zz = (part(c, c, p) for c in range(3))
            xy = part(0, 1, p) + part(1, 0, p)
            xz = part(0, 2, p) + part(2, 0, p)
            yz = grads[(3, "%d%d" % p[1:], "MD"[p[0]])]
            both = xx + yy
            trace = both + zz
            trace = trace * trace
            mix = xx * yy + both * zz
            shear = xy * xy + xz * xz + yz * yz
            if traces is None:
                traces, mixed, shears = trace, mix, shear
            else:
                traces, mixed, shears = traces + trace, mixed + mix, shears + shear
    scale = 1.0 / 1024.0
    return (
        ((LAMBDA + 2.0 * SHEAR_MODULUS) * scale) * traces
        - (4.0 * SHEAR_MODULUS * scale) * mixed
        + (SHEAR_MODULUS * scale) * shears
    )


def z_pass(tile_of, low_of, high_of, along):
    lane = lane_ids()
    tiles = along.shape[1] // 8 - 1
    for c in range(3):
        for t in range(tiles):
            mid = tile_of(c, t)
            low = jnp.where(lane == 0, low_of(c, t), pltpu.roll(mid, 1, 1))
            high = jnp.where(lane == LANES - 1, high_of(c, t), pltpu.roll(mid, LANES - 1, 1))
            for k, v in enumerate(triple(low, mid, high)):
                along[3 * c + k, 8 * t + 8 : 8 * t + 16, :] = v
                if t == tiles - 1:
                    along[3 * c + k, 0:8, :] = v


def rim_shifts(by, t, spot, to_lane):
    n = by // 16
    if t == 2 * n:
        return n, lax.rem(to_lane + LANES - spot, LANES)
    return t % n, lax.rem(to_lane + 2 * LANES - spot - HALF * (t // n), LANES)


def xy_pass(along, ring, slot, emit):
    for t in range(along.shape[1] // 8 - 2):
        rows = slice(8 * t, 8 * t + 8)
        now = {}
        for c in range(3):
            for k, z in enumerate("MDS"):
                three = [along[3 * c + k, 8 * t + 7 + o : 8 * t + 15 + o, :] for o in range(3)]
                values = pair(*three) if z == "S" else triple(*three)
                now.update({(c, y + z): v for y, v in zip("MDS", values)})
        now[(3, "00")] = now[(2, "DM")] + now[(1, "MD")]
        now[(3, "01")] = now[(2, "DD")] + now[(1, "MS")]
        now[(3, "10")] = now[(2, "SM")] + now[(1, "DD")]
        now[(3, "11")] = now[(2, "SD")] + now[(1, "DS")]
        fields = {}
        for f, name in enumerate(FIELDS):
            if name in NO_VALUE or name in ALL_THREE:
                mid = ring[0, f, rows, :]
                after = now[name] - mid
                if emit is not None:
                    fields[name] = mid, ring[1, f, rows, :], after
                ring[0, f, rows, :] = now[name]
                ring[1, f, rows, :] = after
                continue
            if emit is not None:
                fields[name] = ring[slot, f, rows, :], ring[1 - slot, f, rows, :], now[name]
            ring[slot, f, rows, :] = now[name]
        if emit is not None:
            emit(t, energy_of(fields))


def far(axis, index, size):
    at = lax.axis_index(axis) * size + index
    return jnp.minimum(jnp.minimum(at, lax.axis_size(axis) * size - 1 - at), REACH)


def fill_weights(weights):
    table = reach_weights()
    by = weights.shape[1]
    far_z = far("gz", lane_ids(), LANES)
    for d in range(REACH + 1):
        for t in range(by // 8):
            far_y = far("gy", row_ids() + 8 * t, by)
            value = None
            for j in range(REACH, -1, -1):
                line = jnp.full((8, LANES), table[d, j, REACH], F32)
                for k in range(REACH):
                    line = jnp.where(far_z == k, F32(table[d, j, k]), line)
                value = line if value is None else jnp.where(far_y == j, line, value)
            weights[d, 8 * t : 8 * t + 8, :] = value


def inner_kernel(disp, coef, yr1, yr2, rims, inner, partial, weights, along0, along1, ring):
    _, bx, by, _ = disp.shape
    odd_y = is_odd("gy")
    tiles = by // 8
    fill_weights(weights)

    def along_z(x, along):
        def tile_of(c, t):
            if t < tiles:
                return disp[c, x, 8 * t : 8 * t + 8, :]
            return rim_tile(yr1, yr2, c * bx + x, odd_y)

        def rim(side, to_lane):
            def of(c, t):
                tile, turn = rim_shifts(by, t, x, to_lane)
                return pltpu.roll(rims[side * ends_tiles(by) + c * (by // 16 + 1) + tile], turn, 1)

            return of

        z_pass(tile_of, rim(0, 0), rim(1, LANES - 1), along)

    def across(x, along, slot, total):
        totals = [total]

        def emit(t, energy):
            rows = slice(8 * t, 8 * t + 8)
            value = coef[x - 1, rows, :] * energy
            inner[x - 2, rows, :] = value
            totals.append(totals[-1] + weights[far("gx", x - 1, bx), rows, :] * value)

        xy_pass(along, ring, slot, emit if total is not None else None)
        return totals[-1]

    along_z(0, along0)
    along_z(1, along1)
    across(0, along0, 0, None)
    along_z(2, along0)
    across(1, along1, 1, None)

    def planes_two(k, total):
        along_z(2 * k + 1, along1)
        total = across(2 * k, along0, 0, total)
        along_z(jnp.minimum(2 * k + 2, bx - 1), along0)
        return across(2 * k + 1, along1, 1, total)

    partial[...] = lax.fori_loop(1, bx // 2, planes_two, jnp.zeros((8, LANES), F32))


def outer_kernel(
    disp, coef, yr1, yr2, rims, xr1, xr2, inner, partial, weights,
    source, ys1, ys2, sums_out,
    field, rim_coef, ends, total, sums, along0, along1, ring, sem,
):
    _, bx, by, _ = disp.shape
    cells, tall = bx + 2 * REACH, by + 8
    planes, coefs, _ = x_rows(by)
    count = WIDE + 2
    odd_x, odd_y = is_odd("gx"), is_odd("gy")
    row = row_ids()
    for side in range(2):
        def pick(at, size, side=side):
            one, two = xr1[at : at + size, :], cleared("gx", xr2[at : at + size, :])
            return jnp.where(odd_x, two, one) if side else jnp.where(odd_x, one, two)

        for c in range(3):
            for k in range(WIDE):
                field[side, c, k + 2 * side] = pick((c * WIDE + k) * tall, tall)
            for k in range(2):
                x = bx - 2 + k if side else k
                at = k if side else WIDE + k
                field[side, c, at, 0:by, :] = disp[c, x]
                field[side, c, at, by:tall, :] = rim_tile(yr1, yr2, c * bx + x, odd_y)
        for k in range(REACH):
            rim_coef[side, k + side] = pick(planes + k * by, by)
        rim_coef[side, 0 if side else REACH] = coef[bx - 1 if side else 0]
        for j in range(2 * ends_tiles(by)):
            ends[side, j] = pick(coefs + 8 * j, 8)
    for j in range(2 * ends_tiles(by)):
        ends[2, j] = rims[j]
    total[...] = partial[...]

    def one_side(side, carry):
        high_side = side == 1

        def along_z(i, along):
            low_whose = 2 if i >= WIDE else 0
            low_spot = i - WIDE if i >= WIDE else bx - WIDE + i
            high_whose = 2 if i < 2 else 1
            high_spot = bx - 2 + i if i < 2 else i - 2
            whose = jnp.where(high_side, high_whose, low_whose)
            spot = jnp.where(high_side, high_spot, low_spot)

            def rim(z_side, to_lane):
                def of(c, t):
                    tile, turn = rim_shifts(by, t, spot, to_lane)
                    at = z_side * ends_tiles(by) + c * (by // 16 + 1) + tile
                    return pltpu.roll(ends[whose, at], turn, 1)

                return of

            z_pass(
                lambda c, t: field[side, c, i, 8 * t : 8 * t + 8, :],
                rim(0, 0), rim(1, LANES - 1), along,
            )

        alongs = along0, along1
        along_z(0, along0)
        for i in range(count):
            if i + 1 < count:
                along_z(i + 1, alongs[(i + 1) % 2])

            def emit(t, energy, i=i):
                rows = slice(8 * t, 8 * t + 8)
                value = rim_coef[side, i - 2, rows, :] * energy
                source[side * (cells - WIDE) + i - 2, rows, :] = value
                if i in (2, count - 1):
                    own = high_side if i == 2 else jnp.logical_not(high_side)
                    weight = weights[far("gx", bx - 1 if i == 2 else 0, bx), rows, :]
                    total[...] += jnp.where(own, weight * value, 0.0)

            xy_pass(alongs[i % 2], ring, i % 2, emit if i >= 2 else None)
        return carry

    lax.fori_loop(0, 2, one_side, 0)
    sums[...] = jnp.broadcast_to(jnp.sum(total[...], axis=0, keepdims=True), sums.shape)
    leave = pltpu.make_async_copy(sums, sums_out, sem)
    leave.start()


    def copy(x, carry):
        source[x + WIDE] = inner[x]
        return carry

    lax.fori_loop(0, bx - 2, copy, 0, unroll=4)

    def rows_out(q, carry):
        top = row < 4
        first, second = source[2 * q, 0:8, :], source[2 * q + 1, 0:8, :]
        low = jnp.where(top, first, half_turn(second))
        first, second = source[2 * q, by - 8 : by, :], source[2 * q + 1, by - 8 : by, :]
        high = jnp.where(top, half_turn(first), second)
        ys1[q] = jnp.where(odd_y, low, high)
        ys2[q] = jnp.where(odd_y, high, low)
        return carry

    lax.fori_loop(0, cells // 2, rows_out, 0, unroll=6)
    leave.wait()


def pack_columns(source, packed, inside, count):
    cells = source.shape[0]
    top = row_ids() < 4
    for y in range(count):
        tall = jnp.concatenate([source[:, y, :], jnp.zeros((LANES - cells, LANES), F32)], axis=0)
        flat = tall.T
        first, last = flat[0:8], flat[LANES - 8 : LANES]
        packed[y] = jnp.where(top, first, last)
        inside[y] = half_turn(jnp.where(top, last, first))


def pack_kernel(source, both):
    pack_columns(source, both.at[0], both.at[1], source.shape[1])


def corner_kernel(yr1, yr2, both, rim, rim_both, zs1, zs2):
    packed, rim_packed, rim_inside = both.at[0], rim_both.at[0], rim_both.at[1]
    by = packed.shape[0]
    odd_y, odd_z = is_odd("gy"), is_odd("gz")
    top = row_ids() < 4

    def unpack(q, carry):
        one, two = yr1[q], cleared("gy", yr2[q])
        high = jnp.where(odd_y, two, one)
        low = jnp.where(odd_y, one, two)
        rim[2 * q] = jnp.where(top, high, half_turn(low))
        rim[2 * q + 1] = jnp.where(top, half_turn(high), low)
        return carry

    lax.fori_loop(0, yr1.shape[0], unpack, 0, unroll=6)
    pack_columns(rim, rim_packed, rim_inside, 8)

    def send(m, first, second):
        low = jnp.where(top, first, half_turn(second))
        high = jnp.where(top, half_turn(first), second)
        zs1[m] = jnp.where(odd_z, low, high)
        zs2[m] = jnp.where(odd_z, high, low)

    for m in range(by // 2):
        send(m, packed[2 * m], packed[2 * m + 1])
    for m in range(4):
        send(by // 2 + m, rim_packed[2 * m], rim_packed[2 * m + 1])


def sweeps_kernel(source, rim, filtered, work0, work1):
    cells, by, _ = source.shape
    bx = cells - 2 * REACH
    tiles = by // 8
    top = row_ids() < 4
    first_x, last_x = lax.axis_index("gx") == 0, lax.axis_index("gx") == lax.axis_size("gx") - 1
    first_y, last_y = lax.axis_index("gy") == 0, lax.axis_index("gy") == lax.axis_size("gy") - 1

    def put(ref, x, t, value):
        ref[x, 8 * t + 8 : 8 * t + 16, :] = value
        if t == tiles:
            ref[x, 0:8, :] = value
        if t == 0:
            ref[x, by + 16 : by + 24, :] = value

    def begin(x, carry):
        for t in range(tiles):
            put(work0, x, t, POLY[4] * source[x, 8 * t : 8 * t + 8, :])
        put(work0, x, tiles, POLY[4] * rim[x])
        return carry

    lax.fori_loop(0, cells, begin, 0, unroll=8)
    rim_keep = jnp.logical_not(
        jnp.logical_or(
            jnp.logical_and(last_y, top), jnp.logical_and(first_y, jnp.logical_not(top))
        )
    )
    for k in range(4):
        now, later = (work0, work1)[k % 2], (work0, work1)[(k + 1) % 2]

        def sweep(x, k=k, now=now, later=later):
            for t in range(tiles + (k < 3)):
                at = 8 * t + 8
                mid = now[x, at : at + 8, :]
                value = now[x - 1, at : at + 8, :] + now[x + 1, at : at + 8, :]
                value = value + (now[x, at - 1 : at + 7, :] + now[x, at + 1 : at + 9, :])
                value = value + (pltpu.roll(mid, 1, 1) + pltpu.roll(mid, LANES - 1, 1))
                own = source[x, 8 * t : 8 * t + 8, :] if t < tiles else rim[x]
                value = value + POLY[3 - k] * own
                if k == 3:
                    filtered[x - REACH, 8 * t : 8 * t + 8, :] = value
                else:
                    if t == tiles:
                        value = jnp.where(rim_keep, value, 0.0)
                    put(later, x, t, value)

        first, left = (1, cells - 2) if k < 3 else (REACH, bx)
        group = max(g for g in range(2, 36) if left % g == 0)

        def sweeps(j, carry, first=first, group=group, sweep=sweep):
            for g in range(group):
                sweep(first + j * group + g)
            return carry

        lax.fori_loop(0, left // group, sweeps, 0)
        if k < 3:

            @pl.when(first_x)
            def _(later=later):
                later[0:REACH] = jnp.zeros((REACH,) + later.shape[1:], F32)

            @pl.when(last_x)
            def _(later=later):
                later[bx + REACH : cells] = jnp.zeros((REACH,) + later.shape[1:], F32)


def strip_kernel(both, rim_both, zr1, zr2, strip):
    by = both.shape[1]
    tall = by + 8
    packed, inside, rim_packed, rim_inside = both.at[0], both.at[1], rim_both.at[0], rim_both.at[1]
    odd_z, top = is_odd("gz"), row_ids() < 4
    for m in range(tall // 2):
        one, two = zr1[m], cleared("gz", zr2[m])
        low = jnp.where(odd_z, one, two)
        high = jnp.where(odd_z, two, one)
        for part in range(2):
            y = 2 * m + part
            own = half_turn(packed[y] if y < by else rim_packed[y - by])
            strip[y, 0] = jnp.where(top, half_turn(low) if part else low, own)
            strip[y, 1] = jnp.where(top, own, high if part else half_turn(high))
            strip[y, 2] = inside[y] if y < by else rim_inside[y - by]


def finish_kernel(
    count, inner, strip, density, sums,
    projected_out, filtered_out, work0, work1, edges, projected, filtered, sems,
):
    bx, by, _ = density.shape
    tall = by + 8
    lane, row = lane_ids(), row_ids()
    top = row < 4
    first_x, last_x = lax.axis_index("gx") == 0, lax.axis_index("gx") == lax.axis_size("gx") - 1
    first_y, last_y = lax.axis_index("gy") == 0, lax.axis_index("gy") == lax.axis_size("gy") - 1
    first_z, last_z = lax.axis_index("gz") == 0, lax.axis_index("gz") == lax.axis_size("gz") - 1

    inside_x = jnp.logical_not(
        jnp.logical_or(
            jnp.logical_and(first_x, lane < REACH),
            jnp.logical_and(last_x, lane >= bx + REACH),
        )
    )
    keeps = (
        jnp.logical_and(inside_x, jnp.logical_not(jnp.logical_and(first_z, top))),
        jnp.logical_and(
            inside_x, jnp.logical_not(jnp.logical_and(last_z, jnp.logical_not(top)))
        ),
        inside_x,
    )
    work0[...] = POLY[4] * strip[...]
    for k in range(4):
        now, later = (work0, work1)[k % 2], (work0, work1)[(k + 1) % 2]
        for y in range(tall if k < 3 else by):
            low, high, mid = (now[y, part] for part in range(3))
            ups = (
                jnp.where(row == 7, pltpu.roll(mid, 7, 0), pltpu.roll(low, 7, 0)),
                pltpu.roll(high, 7, 0),
                jnp.where(row == 7, pltpu.roll(high, 7, 0), pltpu.roll(mid, 7, 0)),
            )
            downs = (
                pltpu.roll(low, 1, 0),
                jnp.where(row == 0, pltpu.roll(mid, 1, 0), pltpu.roll(high, 1, 0)),
                jnp.where(row == 0, pltpu.roll(low, 1, 0), pltpu.roll(mid, 1, 0)),
            )
            for part in range(3 if k < 3 else 2):
                tile = now[y, part]
                value = now[(y + 1) % tall, part] + now[(y - 1) % tall, part]
                value = value + (pltpu.roll(tile, 1, 1) + pltpu.roll(tile, LANES - 1, 1))
                value = value + (ups[part] + downs[part])
                value = value + POLY[3 - k] * strip[y, part]
                keep = keeps[part]
                if y >= by:
                    outside = first_y if y >= by + 4 else last_y
                    keep = jnp.logical_and(keep, jnp.logical_not(outside))
                later[y, part] = jnp.where(keep, value, 0.0)

    blank = jnp.zeros((LANES - 16, LANES), F32)
    for y in range(by):
        first = half_turn(work0[y, 0])
        last = half_turn(work0[y, 1])
        turned = jnp.concatenate([first, blank, last], axis=0).T
        edges[:, y, :] = turned[0 : bx + 8, :]

    scale = jnp.full((8, LANES), -jnp.sum(sums[...]) / count, F32) + 1e-06
    inverse = 1.0 / scale
    lower = math.tanh(SHARPNESS * THRESHOLD)
    bottom = 1.0 / (lower + math.tanh(SHARPNESS * (1.0 - THRESHOLD)))
    at_face = jnp.logical_or(lane < REACH, lane >= LANES - REACH)

    def project(x, carry):
        for t in range(by // 8):
            rows = slice(8 * t, 8 * t + 8)
            value = jnp.where(at_face, edges[x + REACH, rows, :], inner[x, rows, :])
            filtered[x, rows, :] = value
            trial = density[x, rows, :] - STEP_SIZE * (value * inverse + 1.0)
            level = lower + jnp.tanh(SHARPNESS * (trial - THRESHOLD))
            projected[x, rows, :] = level * bottom
        return carry

    chunks = 4
    size = bx // chunks

    def leave(j):
        at = pl.ds(j * size, size)
        return [
            pltpu.make_async_copy(here.at[at], there.at[at], sems.at[i, j])
            for i, (here, there) in enumerate(
                ((projected, projected_out), (filtered, filtered_out))
            )
        ]

    for j in range(chunks):
        lax.fori_loop(j * size, (j + 1) * size, project, 0, unroll=8)
        for copy in leave(j):
            copy.start()
    for j in range(chunks):
        for copy in leave(j):
            copy.wait()


def call(kernel, outs, scratch=(), cost=0, placed=None):
    return pl.pallas_call(
        kernel,
        out_shape=[jax.ShapeDtypeStruct(s, F32) for s in outs],
        out_specs=placed or [VMEM] * len(outs),
        scratch_shapes=[pltpu.VMEM(s, F32) if isinstance(s, tuple) else s for s in scratch],
        compiler_params=pltpu.CompilerParams(**PARAMS),
        cost_estimate=pl.CostEstimate(flops=cost, bytes_accessed=cost, transcendentals=0),
    )


def body(displacement, density, cell_flags, trim_level):
    bx, by, bz = density.shape
    assert bz == LANES and bx <= HALF and bx % 2 == 0 and by % 16 == 0
    cells, tall = bx + 2 * REACH, by + 8
    devices = lax.axis_size(AXES)
    ys1, ys2 = call(sides_kernel, [(3 * bx, LANES)] * 2)(displacement)
    yr1, yr2 = swap(ys1, ys2, "gy")
    n = 3 * (by // 16)
    low, high = call(faces_kernel, [(n, 8, LANES)] * 2, cost=6_000_000)(displacement)
    zs1, zs2, yr2 = call(ends_kernel, [(n + 1, 8, LANES)] * 2 + [(3 * bx, LANES)])(
        low, high, yr1, yr2
    )
    zr1, zr2 = swap(zs1, zs2, "gz")
    flags_here, zs1 = lax.optimization_barrier((cell_flags, zs1))
    coef = cell_coef(density, flags_here, trim_level)
    brick = (bx, by, LANES)
    rows = x_rows(by)[2]
    xs1, xs2, rims = call(
        outward_kernel, [(rows, LANES), (rows, LANES), (2 * ends_tiles(by), 8, LANES)]
    )(displacement, coef, yr1, yr2, zr1, zr2)
    xr1, xr2 = swap(xs1, xs2, "gx")
    along = (9, by + 16, LANES)
    ring = (2, 24, by, LANES)
    inner, partial, weights = call(
        inner_kernel,
        [(bx - 2, by, LANES), (8, LANES), (REACH + 1, by, LANES)],
        [along, along, ring],
        cost=60_000_000,
    )(displacement, coef, yr1, yr2, rims)
    source, ys1, ys2, sums = call(
        outer_kernel,
        [
            (cells, by, LANES),
            (cells // 2, 8, LANES),
            (cells // 2, 8, LANES),
            (devices, LANES),
        ],
        [
            (2, 3, WIDE + 2, tall, LANES),
            (2, REACH + 1, by, LANES),
            (3, 2 * ends_tiles(by), 8, LANES),
            (8, LANES),
            (devices, LANES),
            along,
            along,
            ring,
            pltpu.SemaphoreType.DMA,
        ],
        placed=[VMEM] * 3 + [ANYWHERE],
    )(displacement, coef, yr1, yr2, rims, xr1, xr2, inner, partial, weights)
    yr1, yr2 = swap(ys1, ys2, "gy")
    (both,) = call(pack_kernel, [(2, by, 8, LANES)], cost=6_000_000)(source)
    sums = lax.all_to_all(sums, AXES, split_axis=0, concat_axis=0, tiled=True)
    rim, rim_both, zs1, zs2 = call(
        corner_kernel,
        [
            (cells, 8, LANES),
            (2, 8, 8, LANES),
            (tall // 2, 8, LANES),
            (tall // 2, 8, LANES),
        ],
    )(yr1, yr2, both)
    zr1, zr2 = swap(zs1, zs2, "gz")
    (middle,) = call(
        sweeps_kernel, [brick], [(cells, by + 24, LANES)] * 2, cost=20_000_000
    )(source, rim)
    strip_shape = (tall, 3, 8, LANES)
    (strip,) = call(strip_kernel, [strip_shape])(both, rim_both, zr1, zr2)
    return call(
        functools.partial(finish_kernel, float(bx * by * bz * devices)),
        [brick, brick],
        [
            strip_shape,
            strip_shape,
            (bx + 8, by, LANES),
            brick,
            brick,
            pltpu.SemaphoreType.DMA((2, 4)),
        ],
        placed=[ANYWHERE] * 2,
    )(middle, strip, density, sums)


def solution(mesh):
    return jax.shard_map(
        body,
        mesh=mesh,
        in_specs=(P(None, *AXES), P(*AXES), P(*AXES), P(*AXES)),
        out_specs=(P(*AXES), P(*AXES)),
        check_vma=False,
    )
```

```python
import functools
import math

import jax
import jax.numpy as jnp
import numpy as np
from jax import lax
from jax.experimental import pallas as pl
from jax.experimental.pallas import tpu as pltpu
from jax.sharding import PartitionSpec as P

LAMBDA = 0.3 / 0.52
SHEAR_MODULUS = 1.0 / 2.6
SPREAD_MID = 5.5
SPREAD_HALF = 4.5
STEP_SIZE = 0.3
SHARPNESS = 8.0
THRESHOLD = 0.5

AXES = ("gx", "gy", "gz")
LANES = 128
HALF = 64
REACH = 4
WIDE = REACH + 1

SIGMA = SPREAD_MID / SPREAD_HALF
CHEB = 16.0 * SIGMA**5 - 20.0 * SIGMA**3 + 5.0 * SIGMA
POLY = [
    (16.0 * SIGMA**4 - 20.0 * SIGMA**2 + 5.0) / (SPREAD_HALF * CHEB),
    (16.0 * SIGMA**3 - 20.0 * SIGMA) / 6.0 / (SPREAD_HALF * CHEB),
    (16.0 * SIGMA**2 - 20.0) / 36.0 / (SPREAD_HALF * CHEB),
    16.0 * SIGMA / 216.0 / (SPREAD_HALF * CHEB),
    16.0 / 1296.0 / (SPREAD_HALF * CHEB),
]


def reach_weights():
    power = np.ones((5 + REACH,) * 3)
    total = POLY[0] * power
    for m in range(1, REACH + 1):
        wide = np.pad(np.pad(power, ((0, 1),) * 3, mode="edge"), ((1, 0),) * 3)
        power = sum(
            np.roll(wide, step, dim)[1:-1, 1:-1, 1:-1] for dim in range(3) for step in (1, -1)
        )
        total = total + POLY[m] * power
    return total[:5, :5, :5]


F32 = jnp.float32
VMEM = pl.BlockSpec(memory_space=pltpu.VMEM)
ANYWHERE = pl.BlockSpec(memory_space=pl.ANY)
PARAMS = dict(vmem_limit_bytes=20 * 1024 * 1024)


def partners(axis, sizes):
    dim = AXES.index(axis)
    count, near = sizes[dim], 1 if axis == "gz" else 2
    first, second = [], []
    for at in np.ndindex(*sizes):
        for pairs, other in (
            (first, at[dim] ^ 1),
            (second, at[dim] + 1 if at[dim] % 2 else at[dim] - 1),
        ):
            to = list(at)
            if 0 <= other < count:
                to[dim] = other
            elif sizes[near] > 1:
                to[near] ^= 1
            pairs.append(tuple(int(np.ravel_multi_index(v, sizes)) for v in (at, to)))
    return first, second


def swap(first, second, axis):
    sizes = tuple(lax.axis_size(a) for a in AXES)
    near, far_ones = partners(axis, sizes)
    return lax.ppermute(first, AXES, near), lax.ppermute(second, AXES, far_ones)


def at_end(axis):
    at = lax.axis_index(axis)
    return jnp.logical_or(at == 0, at == lax.axis_size(axis) - 1)


def cleared(axis, value):
    return jnp.where(at_end(axis), 0.0, value)


def is_odd(axis):
    return lax.rem(lax.axis_index(axis), 2) == 1


def cell_coef(density, cell_flags, trim_level):
    trimmed = (1.0 + trim_level.astype(F32)) * 0.2
    share = jnp.where(cell_flags == 1, 1.0, jnp.where(cell_flags == 2, trimmed, 0.001))
    return -3.0 * density * density * density * share


def lane_ids():
    return lax.broadcasted_iota(jnp.int32, (8, LANES), 1)


def row_ids():
    return lax.broadcasted_iota(jnp.int32, (8, LANES), 0)


def half_turn(tile):
    return pltpu.roll(tile, 4, 0)


def rim_tile(first, second, index, odd):
    one = jnp.broadcast_to(first[pl.ds(index, 1), :], (8, LANES))
    two = jnp.broadcast_to(second[pl.ds(index, 1), :], (8, LANES))
    at_top = row_ids() == 0
    return jnp.where(jnp.logical_xor(at_top, odd), one, two)


def two_halves(first, second):
    spare = HALF - first.shape[0]
    if spare:
        zero = jnp.zeros((spare, LANES), F32)
        first = jnp.concatenate([first, zero], axis=0)
        second = jnp.concatenate([second, zero], axis=0)
    return jnp.concatenate([first, second], axis=0).T


def sides_kernel(disp, ys1, ys2):
    _, bx, by, _ = disp.shape
    odd_y = is_odd("gy")
    for c in range(3):
        rows = slice(c * bx, c * bx + bx)
        low, high = disp[c, :, 0, :], disp[c, :, by - 1, :]
        ys1[rows, :] = jnp.where(odd_y, low, high)
        ys2[rows, :] = jnp.where(odd_y, high, low)


def faces_kernel(disp, low, high):
    _, _, by, _ = disp.shape
    n = by // 16
    for c in range(3):
        for y in range(by // 2):
            turned = two_halves(disp[c, :, y, :], disp[c, :, y + by // 2, :])
            low[c * n + y // 8, y % 8 : y % 8 + 1, :] = turned[0:1]
            high[c * n + y // 8, y % 8 : y % 8 + 1, :] = turned[LANES - 1 : LANES]


def ends_kernel(low, high, yr1, yr2_raw, zs1, zs2, yr2):
    odd_z = is_odd("gz")
    n, bx = low.shape[0], yr1.shape[0] // 3
    yr2[...] = cleared("gy", yr2_raw[...])
    zs1[0:n] = jnp.where(odd_z, low[...], high[...])
    zs2[0:n] = jnp.where(odd_z, high[...], low[...])
    zs1[n] = jnp.zeros((8, LANES), F32)
    zs2[n] = jnp.zeros((8, LANES), F32)
    for c in range(3):
        rows = slice(c * bx, c * bx + bx)
        turned = two_halves(yr1[rows, :], yr2[rows, :])
        near, far = turned[0:1], turned[LANES - 1 : LANES]
        zs1[n, c : c + 1, :] = jnp.where(odd_z, near, far)
        zs2[n, c : c + 1, :] = jnp.where(odd_z, far, near)


def x_rows(by):
    tall = by + 8
    planes = 3 * WIDE * tall
    coefs = planes + REACH * by
    return planes, coefs, coefs + 2 * 3 * (by // 16 + 1) * 8


def ends_tiles(by):
    return 3 * (by // 16 + 1)


def outward_kernel(disp, coef, yr1, yr2, zr1, zr2, xs1, xs2, rims):
    _, bx, by, _ = disp.shape
    tall, n = by + 8, by // 16
    odd_x, odd_y, odd_z = is_odd("gx"), is_odd("gy"), is_odd("gz")
    top_row, left = row_ids() == 0, lane_ids() < HALF
    for side in range(2):
        def pick(*at, side=side):
            one, two = zr1[at], cleared("gz", zr2[at])
            return jnp.where(odd_z, two, one) if side else jnp.where(odd_z, one, two)

        for c in range(3):
            base = side * ends_tiles(by) + c * (n + 1)
            for t in range(n):
                rims[base + t] = pick(c * n + t)
            both = jnp.broadcast_to(pick(3 * n, slice(c, c + 1), slice(None)), (8, LANES))
            other = pltpu.roll(both, HALF, 1)
            rims[base + n] = jnp.where(jnp.logical_xor(top_row, odd_y), both, other)
    planes, coefs, _ = x_rows(by)
    for out, at_low in ((xs1, odd_x), (xs2, jnp.logical_not(odd_x))):
        start = jnp.where(at_low, 0, bx - WIDE)
        for c in range(3):
            for k in range(WIDE):
                at = (c * WIDE + k) * tall
                out[at : at + by, :] = disp[c, start + k]
                out[at + by : at + tall, :] = rim_tile(yr1, yr2, c * bx + start + k, odd_y)
        start = jnp.where(at_low, 0, bx - REACH)
        for k in range(REACH):
            out[planes + k * by : planes + (k + 1) * by, :] = coef[start + k]
        for j in range(2 * ends_tiles(by)):
            out[coefs + 8 * j : coefs + 8 * j + 8, :] = rims[j]


def triple(a, b, c):
    ends = a + c
    curve = ends - 2.0 * b
    return 4.0 * b + (2.0 / 3.0) * curve, c - a, curve


def pair(a, b, c):
    return (2.0 / 3.0) * (a + c) + (8.0 / 3.0) * b, c - a


FIELDS = (
    [(0, key) for key in ("MM", "MD", "MS", "DM", "DD", "DS", "SM", "SD")]
    + [(1, key) for key in ("MM", "MD", "DM", "DD", "SM", "SD")]
    + [(2, key) for key in ("MM", "MD", "DM", "DD", "MS", "DS")]
    + [(3, key) for key in ("00", "01", "10", "11")]
)
ALL_THREE = {(0, "MD"), (0, "DM"), (0, "DD"), (1, "DM"), (1, "DD"), (2, "MD"), (2, "DD")}
NO_VALUE = {(0, "MM"), (1, "MM"), (1, "MD"), (2, "MM"), (2, "DM")}


def energy_of(fields):
    grads = {}
    for name, planes in fields.items():
        if name in NO_VALUE or name in ALL_THREE:
            mid, before, after = planes
            curve = after - before
            grads[name + ("D",)], grads[name + ("S",)] = before + after, curve
            if name in ALL_THREE:
                grads[name + ("M",)] = 4.0 * mid + (2.0 / 3.0) * curve
        else:
            grads.update({name + (x,): v for x, v in zip("MD", pair(*planes))})
    names = "MD", "DS"

    def part(c, e, p):
        ops = [names[1 if d == e else 0][p[d]] for d in range(3)]
        return grads[(c, ops[1] + ops[2], ops[0])]

    traces = mixed = shears = None
    for order in (3, 2, 1, 0):
        if traces is not None:
            traces, mixed, shears = (v * (1.0 / 3.0) for v in (traces, mixed, shears))
        for bits in range(8):
            p = (bits >> 2) & 1, (bits >> 1) & 1, bits & 1
            if sum(p) != order:
                continue
            xx, yy, zz = (part(c, c, p) for c in range(3))
            xy = part(0, 1, p) + part(1, 0, p)
            xz = part(0, 2, p) + part(2, 0, p)
            yz = grads[(3, "%d%d" % p[1:], "MD"[p[0]])]
            both = xx + yy
            trace = both + zz
            trace = trace * trace
            mix = xx * yy + both * zz
            shear = xy * xy + xz * xz + yz * yz
            if traces is None:
                traces, mixed, shears = trace, mix, shear
            else:
                traces, mixed, shears = traces + trace, mixed + mix, shears + shear
    scale = 1.0 / 1024.0
    return (
        ((LAMBDA + 2.0 * SHEAR_MODULUS) * scale) * traces
        - (4.0 * SHEAR_MODULUS * scale) * mixed
        + (SHEAR_MODULUS * scale) * shears
    )


def z_pass(tile_of, low_of, high_of, along):
    lane = lane_ids()
    tiles = along.shape[1] // 8 - 1
    for c in range(3):
        for t in range(tiles):
            mid = tile_of(c, t)
            low = jnp.where(lane == 0, low_of(c, t), pltpu.roll(mid, 1, 1))
            high = jnp.where(lane == LANES - 1, high_of(c, t), pltpu.roll(mid, LANES - 1, 1))
            for k, v in enumerate(triple(low, mid, high)):
                along[3 * c + k, 8 * t + 8 : 8 * t + 16, :] = v
                if t == tiles - 1:
                    along[3 * c + k, 0:8, :] = v


def rim_shifts(by, t, spot, to_lane):
    n = by // 16
    if t == 2 * n:
        return n, lax.rem(to_lane + LANES - spot, LANES)
    return t % n, lax.rem(to_lane + 2 * LANES - spot - HALF * (t // n), LANES)


def xy_pass(along, ring, slot, emit, keep=True):
    for t in range(along.shape[1] // 8 - 2):
        rows = slice(8 * t, 8 * t + 8)
        now = {}
        for c in range(3):
            for k, z in enumerate("MDS"):
                three = [along[3 * c + k, 8 * t + 7 + o : 8 * t + 15 + o, :] for o in range(3)]
                values = pair(*three) if z == "S" else triple(*three)
                now.update({(c, y + z): v for y, v in zip("MDS", values)})
        now[(3, "00")] = now[(2, "DM")] + now[(1, "MD")]
        now[(3, "01")] = now[(2, "DD")] + now[(1, "MS")]
        now[(3, "10")] = now[(2, "SM")] + now[(1, "DD")]
        now[(3, "11")] = now[(2, "SD")] + now[(1, "DS")]
        fields = {}
        for f, name in enumerate(FIELDS):
            steps = name in NO_VALUE or name in ALL_THREE
            if steps and keep:
                mid = ring[0, f, rows, :]
                after = now[name] - mid
                if emit is not None:
                    fields[name] = mid, ring[1, f, rows, :], after
                ring[0, f, rows, :] = now[name]
                ring[1, f, rows, :] = after
                continue
            if emit is not None:
                old, mid = ring[slot, f, rows, :], ring[1 - slot, f, rows, :]
                fields[name] = old, mid, now[name]
                if steps:
                    fields[name] = mid, mid - old, now[name] - mid
            ring[slot, f, rows, :] = now[name]
        if emit is not None:
            emit(t, energy_of(fields))


def far(axis, index, size):
    at = lax.axis_index(axis) * size + index
    return jnp.minimum(jnp.minimum(at, lax.axis_size(axis) * size - 1 - at), REACH)


def fill_weights(weights):
    table = reach_weights()
    by = weights.shape[1]
    far_z = far("gz", lane_ids(), LANES)
    for d in range(REACH + 1):
        for t in range(by // 8):
            far_y = far("gy", row_ids() + 8 * t, by)
            value = None
            for j in range(REACH, -1, -1):
                line = jnp.full((8, LANES), table[d, j, REACH], F32)
                for k in range(REACH):
                    line = jnp.where(far_z == k, F32(table[d, j, k]), line)
                value = line if value is None else jnp.where(far_y == j, line, value)
            weights[d, 8 * t : 8 * t + 8, :] = value


def inner_kernel(disp, coef, yr1, yr2, rims, inner, partial, weights, along0, along1, ring):
    _, bx, by, _ = disp.shape
    odd_y = is_odd("gy")
    tiles = by // 8
    fill_weights(weights)

    def along_z(x, along):
        def tile_of(c, t):
            if t < tiles:
                return disp[c, x, 8 * t : 8 * t + 8, :]
            return rim_tile(yr1, yr2, c * bx + x, odd_y)

        def rim(side, to_lane):
            def of(c, t):
                tile, turn = rim_shifts(by, t, x, to_lane)
                return pltpu.roll(rims[side * ends_tiles(by) + c * (by // 16 + 1) + tile], turn, 1)

            return of

        z_pass(tile_of, rim(0, 0), rim(1, LANES - 1), along)

    def across(x, along, slot, total):
        totals = [total]

        def emit(t, energy):
            rows = slice(8 * t, 8 * t + 8)
            value = coef[x - 1, rows, :] * energy
            inner[x - 2, rows, :] = value
            totals.append(totals[-1] + weights[far("gx", x - 1, bx), rows, :] * value)

        xy_pass(along, ring, slot, emit if total is not None else None)
        return totals[-1]

    along_z(0, along0)
    along_z(1, along1)
    across(0, along0, 0, None)
    along_z(2, along0)
    across(1, along1, 1, None)

    def planes_two(k, total):
        along_z(2 * k + 1, along1)
        total = across(2 * k, along0, 0, total)
        along_z(jnp.minimum(2 * k + 2, bx - 1), along0)
        return across(2 * k + 1, along1, 1, total)

    partial[...] = lax.fori_loop(1, bx // 2, planes_two, jnp.zeros((8, LANES), F32))


def outer_kernel(
    disp, coef, yr1, yr2, rims, xr1, xr2, inner, partial, weights,
    source, ys1, ys2, sums_out,
    field, rim_coef, ends, total, sums, along0, along1, ring, sem,
):
    _, bx, by, _ = disp.shape
    cells, tall = bx + 2 * REACH, by + 8
    planes, coefs, _ = x_rows(by)
    count = WIDE + 2
    odd_x, odd_y = is_odd("gx"), is_odd("gy")
    row = row_ids()
    for side in range(2):
        def pick(at, size, side=side):
            one, two = xr1[at : at + size, :], cleared("gx", xr2[at : at + size, :])
            return jnp.where(odd_x, two, one) if side else jnp.where(odd_x, one, two)

        for c in range(3):
            for k in range(WIDE):
                field[side, c, k + 2 * side] = pick((c * WIDE + k) * tall, tall)
            for k in range(2):
                x = bx - 2 + k if side else k
                at = k if side else WIDE + k
                field[side, c, at, 0:by, :] = disp[c, x]
                field[side, c, at, by:tall, :] = rim_tile(yr1, yr2, c * bx + x, odd_y)
        for k in range(REACH):
            rim_coef[side, k + side] = pick(planes + k * by, by)
        rim_coef[side, 0 if side else REACH] = coef[bx - 1 if side else 0]
        for j in range(2 * ends_tiles(by)):
            ends[side, j] = pick(coefs + 8 * j, 8)
    for j in range(2 * ends_tiles(by)):
        ends[2, j] = rims[j]
    total[...] = partial[...]

    def one_side(side, carry):
        high_side = side == 1

        def along_z(i, along):
            low_whose = 2 if i >= WIDE else 0
            low_spot = i - WIDE if i >= WIDE else bx - WIDE + i
            high_whose = 2 if i < 2 else 1
            high_spot = bx - 2 + i if i < 2 else i - 2
            whose = jnp.where(high_side, high_whose, low_whose)
            spot = jnp.where(high_side, high_spot, low_spot)

            def rim(z_side, to_lane):
                def of(c, t):
                    tile, turn = rim_shifts(by, t, spot, to_lane)
                    at = z_side * ends_tiles(by) + c * (by // 16 + 1) + tile
                    return pltpu.roll(ends[whose, at], turn, 1)

                return of

            z_pass(
                lambda c, t: field[side, c, i, 8 * t : 8 * t + 8, :],
                rim(0, 0), rim(1, LANES - 1), along,
            )

        alongs = along0, along1
        along_z(0, along0)
        for i in range(count):
            if i + 1 < count:
                along_z(i + 1, alongs[(i + 1) % 2])

            def emit(t, energy, i=i):
                rows = slice(8 * t, 8 * t + 8)
                value = rim_coef[side, i - 2, rows, :] * energy
                source[side * (cells - WIDE) + i - 2, rows, :] = value
                if i in (2, count - 1):
                    own = high_side if i == 2 else jnp.logical_not(high_side)
                    weight = weights[far("gx", bx - 1 if i == 2 else 0, bx), rows, :]
                    total[...] += jnp.where(own, weight * value, 0.0)

            xy_pass(alongs[i % 2], ring, i % 2, emit if i >= 2 else None, keep=False)
        return carry

    lax.fori_loop(0, 2, one_side, 0)
    sums[...] = jnp.broadcast_to(jnp.sum(total[...], axis=0, keepdims=True), sums.shape)
    leave = pltpu.make_async_copy(sums, sums_out, sem)
    leave.start()


    def copy(x, carry):
        source[x + WIDE] = inner[x]
        return carry

    lax.fori_loop(0, bx - 2, copy, 0, unroll=4)

    def rows_out(q, carry):
        top = row < 4
        first, second = source[2 * q, 0:8, :], source[2 * q + 1, 0:8, :]
        low = jnp.where(top, first, half_turn(second))
        first, second = source[2 * q, by - 8 : by, :], source[2 * q + 1, by - 8 : by, :]
        high = jnp.where(top, half_turn(first), second)
        ys1[q] = jnp.where(odd_y, low, high)
        ys2[q] = jnp.where(odd_y, high, low)
        return carry

    lax.fori_loop(0, cells // 2, rows_out, 0, unroll=6)
    leave.wait()


def pack_columns(source, packed, inside, count):
    cells = source.shape[0]
    top = row_ids() < 4
    for y in range(count):
        tall = jnp.concatenate([source[:, y, :], jnp.zeros((LANES - cells, LANES), F32)], axis=0)
        flat = tall.T
        first, last = flat[0:8], flat[LANES - 8 : LANES]
        packed[y] = jnp.where(top, first, last)
        inside[y] = half_turn(jnp.where(top, last, first))


def pack_kernel(source, both):
    pack_columns(source, both.at[0], both.at[1], source.shape[1])


def corner_kernel(yr1, yr2, both, rim, rim_both, zs1, zs2):
    packed, rim_packed, rim_inside = both.at[0], rim_both.at[0], rim_both.at[1]
    by = packed.shape[0]
    odd_y, odd_z = is_odd("gy"), is_odd("gz")
    top = row_ids() < 4

    def unpack(q, carry):
        one, two = yr1[q], cleared("gy", yr2[q])
        high = jnp.where(odd_y, two, one)
        low = jnp.where(odd_y, one, two)
        rim[2 * q] = jnp.where(top, high, half_turn(low))
        rim[2 * q + 1] = jnp.where(top, half_turn(high), low)
        return carry

    lax.fori_loop(0, yr1.shape[0], unpack, 0, unroll=6)
    pack_columns(rim, rim_packed, rim_inside, 8)

    def send(m, first, second):
        low = jnp.where(top, first, half_turn(second))
        high = jnp.where(top, half_turn(first), second)
        zs1[m] = jnp.where(odd_z, low, high)
        zs2[m] = jnp.where(odd_z, high, low)

    for m in range(by // 2):
        send(m, packed[2 * m], packed[2 * m + 1])
    for m in range(4):
        send(by // 2 + m, rim_packed[2 * m], rim_packed[2 * m + 1])


def sweeps_kernel(source, rim, filtered, work0, work1):
    cells, by, _ = source.shape
    bx = cells - 2 * REACH
    tiles = by // 8
    top = row_ids() < 4
    first_x, last_x = lax.axis_index("gx") == 0, lax.axis_index("gx") == lax.axis_size("gx") - 1
    first_y, last_y = lax.axis_index("gy") == 0, lax.axis_index("gy") == lax.axis_size("gy") - 1

    def put(ref, x, t, value):
        ref[x, 8 * t + 8 : 8 * t + 16, :] = value
        if t == tiles:
            ref[x, 0:8, :] = value
        if t == 0:
            ref[x, by + 16 : by + 24, :] = value

    def begin(x, carry):
        for t in range(tiles):
            put(work0, x, t, POLY[4] * source[x, 8 * t : 8 * t + 8, :])
        put(work0, x, tiles, POLY[4] * rim[x])
        return carry

    lax.fori_loop(0, cells, begin, 0, unroll=8)
    rim_keep = jnp.logical_not(
        jnp.logical_or(
            jnp.logical_and(last_y, top), jnp.logical_and(first_y, jnp.logical_not(top))
        )
    )
    for k in range(4):
        now, later = (work0, work1)[k % 2], (work0, work1)[(k + 1) % 2]

        def sweep(x, k=k, now=now, later=later):
            for t in range(tiles + (k < 3)):
                at = 8 * t + 8
                mid = now[x, at : at + 8, :]
                value = now[x - 1, at : at + 8, :] + now[x + 1, at : at + 8, :]
                value = value + (now[x, at - 1 : at + 7, :] + now[x, at + 1 : at + 9, :])
                value = value + (pltpu.roll(mid, 1, 1) + pltpu.roll(mid, LANES - 1, 1))
                own = source[x, 8 * t : 8 * t + 8, :] if t < tiles else rim[x]
                value = value + POLY[3 - k] * own
                if k == 3:
                    filtered[x - REACH, 8 * t : 8 * t + 8, :] = value
                else:
                    if t == tiles:
                        value = jnp.where(rim_keep, value, 0.0)
                    put(later, x, t, value)

        first, left = (1, cells - 2) if k < 3 else (REACH, bx)
        group = max(g for g in range(2, 36) if left % g == 0)

        def sweeps(j, carry, first=first, group=group, sweep=sweep):
            for g in range(group):
                sweep(first + j * group + g)
            return carry

        lax.fori_loop(0, left // group, sweeps, 0)
        if k < 3:

            @pl.when(first_x)
            def _(later=later):
                later[0:REACH] = jnp.zeros((REACH,) + later.shape[1:], F32)

            @pl.when(last_x)
            def _(later=later):
                later[bx + REACH : cells] = jnp.zeros((REACH,) + later.shape[1:], F32)


def strip_kernel(both, rim_both, zr1, zr2, strip):
    by = both.shape[1]
    tall = by + 8
    packed, inside, rim_packed, rim_inside = both.at[0], both.at[1], rim_both.at[0], rim_both.at[1]
    odd_z, top = is_odd("gz"), row_ids() < 4
    for m in range(tall // 2):
        one, two = zr1[m], cleared("gz", zr2[m])
        low = jnp.where(odd_z, one, two)
        high = jnp.where(odd_z, two, one)
        for part in range(2):
            y = 2 * m + part
            own = half_turn(packed[y] if y < by else rim_packed[y - by])
            strip[y, 0] = jnp.where(top, half_turn(low) if part else low, own)
            strip[y, 1] = jnp.where(top, own, high if part else half_turn(high))
            strip[y, 2] = inside[y] if y < by else rim_inside[y - by]


def finish_kernel(
    count, inner, strip, density, sums,
    projected_out, filtered_out, work0, work1, edges, projected, filtered, sems,
):
    bx, by, _ = density.shape
    tall = by + 8
    lane, row = lane_ids(), row_ids()
    top = row < 4
    first_x, last_x = lax.axis_index("gx") == 0, lax.axis_index("gx") == lax.axis_size("gx") - 1
    first_y, last_y = lax.axis_index("gy") == 0, lax.axis_index("gy") == lax.axis_size("gy") - 1
    first_z, last_z = lax.axis_index("gz") == 0, lax.axis_index("gz") == lax.axis_size("gz") - 1

    inside_x = jnp.logical_not(
        jnp.logical_or(
            jnp.logical_and(first_x, lane < REACH),
            jnp.logical_and(last_x, lane >= bx + REACH),
        )
    )
    keeps = (
        jnp.logical_and(inside_x, jnp.logical_not(jnp.logical_and(first_z, top))),
        jnp.logical_and(
            inside_x, jnp.logical_not(jnp.logical_and(last_z, jnp.logical_not(top)))
        ),
        inside_x,
    )
    work0[...] = POLY[4] * strip[...]
    for k in range(4):
        now, later = (work0, work1)[k % 2], (work0, work1)[(k + 1) % 2]
        for y in range(tall if k < 3 else by):
            low, high, mid = (now[y, part] for part in range(3))
            ups = (
                jnp.where(row == 7, pltpu.roll(mid, 7, 0), pltpu.roll(low, 7, 0)),
                pltpu.roll(high, 7, 0),
                jnp.where(row == 7, pltpu.roll(high, 7, 0), pltpu.roll(mid, 7, 0)),
            )
            downs = (
                pltpu.roll(low, 1, 0),
                jnp.where(row == 0, pltpu.roll(mid, 1, 0), pltpu.roll(high, 1, 0)),
                jnp.where(row == 0, pltpu.roll(low, 1, 0), pltpu.roll(mid, 1, 0)),
            )
            for part in range(3 if k < 3 else 2):
                tile = now[y, part]
                value = now[(y + 1) % tall, part] + now[(y - 1) % tall, part]
                value = value + (pltpu.roll(tile, 1, 1) + pltpu.roll(tile, LANES - 1, 1))
                value = value + (ups[part] + downs[part])
                value = value + POLY[3 - k] * strip[y, part]
                keep = keeps[part]
                if y >= by:
                    outside = first_y if y >= by + 4 else last_y
                    keep = jnp.logical_and(keep, jnp.logical_not(outside))
                later[y, part] = jnp.where(keep, value, 0.0)

    blank = jnp.zeros((LANES - 16, LANES), F32)
    for y in range(by):
        first = half_turn(work0[y, 0])
        last = half_turn(work0[y, 1])
        turned = jnp.concatenate([first, blank, last], axis=0).T
        edges[:, y, :] = turned[0 : bx + 8, :]

    scale = jnp.full((8, LANES), -jnp.sum(sums[...]) / count, F32) + 1e-06
    inverse = 1.0 / scale
    lower = math.tanh(SHARPNESS * THRESHOLD)
    bottom = 1.0 / (lower + math.tanh(SHARPNESS * (1.0 - THRESHOLD)))
    at_face = jnp.logical_or(lane < REACH, lane >= LANES - REACH)

    def project(x, carry):
        for t in range(by // 8):
            rows = slice(8 * t, 8 * t + 8)
            value = jnp.where(at_face, edges[x + REACH, rows, :], inner[x, rows, :])
            filtered[x, rows, :] = value
            trial = density[x, rows, :] - STEP_SIZE * (value * inverse + 1.0)
            level = lower + jnp.tanh(SHARPNESS * (trial - THRESHOLD))
            projected[x, rows, :] = level * bottom
        return carry

    chunks = 4
    size = bx // chunks

    def leave(j):
        at = pl.ds(j * size, size)
        return [
            pltpu.make_async_copy(here.at[at], there.at[at], sems.at[i, j])
            for i, (here, there) in enumerate(
                ((projected, projected_out), (filtered, filtered_out))
            )
        ]

    for j in range(chunks):
        lax.fori_loop(j * size, (j + 1) * size, project, 0, unroll=8)
        for copy in leave(j):
            copy.start()
    for j in range(chunks):
        for copy in leave(j):
            copy.wait()


def call(kernel, outs, scratch=(), cost=0, placed=None):
    return pl.pallas_call(
        kernel,
        out_shape=[jax.ShapeDtypeStruct(s, F32) for s in outs],
        out_specs=placed or [VMEM] * len(outs),
        scratch_shapes=[pltpu.VMEM(s, F32) if isinstance(s, tuple) else s for s in scratch],
        compiler_params=pltpu.CompilerParams(**PARAMS),
        cost_estimate=pl.CostEstimate(flops=cost, bytes_accessed=cost, transcendentals=0),
    )


def body(displacement, density, cell_flags, trim_level):
    bx, by, bz = density.shape
    assert bz == LANES and bx <= HALF and bx % 2 == 0 and by % 16 == 0
    cells, tall = bx + 2 * REACH, by + 8
    devices = lax.axis_size(AXES)
    ys1, ys2 = call(sides_kernel, [(3 * bx, LANES)] * 2)(displacement)
    yr1, yr2 = swap(ys1, ys2, "gy")
    n = 3 * (by // 16)
    low, high = call(faces_kernel, [(n, 8, LANES)] * 2, cost=6_000_000)(displacement)
    flags_here, low = lax.optimization_barrier((cell_flags, low))
    coef = cell_coef(density, flags_here, trim_level)
    coef, low = lax.optimization_barrier((coef, low))
    zs1, zs2, yr2 = call(ends_kernel, [(n + 1, 8, LANES)] * 2 + [(3 * bx, LANES)])(
        low, high, yr1, yr2
    )
    zr1, zr2 = swap(zs1, zs2, "gz")
    brick = (bx, by, LANES)
    rows = x_rows(by)[2]
    xs1, xs2, rims = call(
        outward_kernel, [(rows, LANES), (rows, LANES), (2 * ends_tiles(by), 8, LANES)]
    )(displacement, coef, yr1, yr2, zr1, zr2)
    xr1, xr2 = swap(xs1, xs2, "gx")
    along = (9, by + 16, LANES)
    ring = (2, 24, by, LANES)
    inner, partial, weights = call(
        inner_kernel,
        [(bx - 2, by, LANES), (8, LANES), (REACH + 1, by, LANES)],
        [along, along, ring],
        cost=60_000_000,
    )(displacement, coef, yr1, yr2, rims)
    source, ys1, ys2, sums = call(
        outer_kernel,
        [
            (cells, by, LANES),
            (cells // 2, 8, LANES),
            (cells // 2, 8, LANES),
            (devices, LANES),
        ],
        [
            (2, 3, WIDE + 2, tall, LANES),
            (2, REACH + 1, by, LANES),
            (3, 2 * ends_tiles(by), 8, LANES),
            (8, LANES),
            (devices, LANES),
            along,
            along,
            ring,
            pltpu.SemaphoreType.DMA,
        ],
        placed=[VMEM] * 3 + [ANYWHERE],
    )(displacement, coef, yr1, yr2, rims, xr1, xr2, inner, partial, weights)
    yr1, yr2 = swap(ys1, ys2, "gy")
    (both,) = call(pack_kernel, [(2, by, 8, LANES)], cost=6_000_000)(source)
    sums = lax.all_to_all(sums, AXES, split_axis=0, concat_axis=0, tiled=True)
    rim, rim_both, zs1, zs2 = call(
        corner_kernel,
        [
            (cells, 8, LANES),
            (2, 8, 8, LANES),
            (tall // 2, 8, LANES),
            (tall // 2, 8, LANES),
        ],
    )(yr1, yr2, both)
    zr1, zr2 = swap(zs1, zs2, "gz")
    (middle,) = call(
        sweeps_kernel, [brick], [(cells, by + 24, LANES)] * 2, cost=20_000_000
    )(source, rim)
    strip_shape = (tall, 3, 8, LANES)
    (strip,) = call(strip_kernel, [strip_shape])(both, rim_both, zr1, zr2)
    return call(
        functools.partial(finish_kernel, float(bx * by * bz * devices)),
        [brick, brick],
        [
            strip_shape,
            strip_shape,
            (bx + 8, by, LANES),
            brick,
            brick,
            pltpu.SemaphoreType.DMA((2, 4)),
        ],
        placed=[ANYWHERE] * 2,
    )(middle, strip, density, sums)


def solution(mesh):
    return jax.shard_map(
        body,
        mesh=mesh,
        in_specs=(P(None, *AXES), P(*AXES), P(*AXES), P(*AXES)),
        out_specs=(P(*AXES), P(*AXES)),
        check_vma=False,
    )
```

```python
import functools
import math

import jax
import jax.numpy as jnp
import numpy as np
from jax import lax
from jax.experimental import pallas as pl
from jax.experimental.pallas import tpu as pltpu
from jax.sharding import PartitionSpec as P

LAMBDA = 0.3 / 0.52
SHEAR_MODULUS = 1.0 / 2.6
SPREAD_MID = 5.5
SPREAD_HALF = 4.5
STEP_SIZE = 0.3
SHARPNESS = 8.0
THRESHOLD = 0.5

AXES = ("gx", "gy", "gz")
LANES = 128
HALF = 64
REACH = 4
WIDE = REACH + 1

SIGMA = SPREAD_MID / SPREAD_HALF
CHEB = 16.0 * SIGMA**5 - 20.0 * SIGMA**3 + 5.0 * SIGMA
POLY = [
    (16.0 * SIGMA**4 - 20.0 * SIGMA**2 + 5.0) / (SPREAD_HALF * CHEB),
    (16.0 * SIGMA**3 - 20.0 * SIGMA) / 6.0 / (SPREAD_HALF * CHEB),
    (16.0 * SIGMA**2 - 20.0) / 36.0 / (SPREAD_HALF * CHEB),
    16.0 * SIGMA / 216.0 / (SPREAD_HALF * CHEB),
    16.0 / 1296.0 / (SPREAD_HALF * CHEB),
]


def reach_weights():
    power = np.ones((5 + REACH,) * 3)
    total = POLY[0] * power
    for m in range(1, REACH + 1):
        wide = np.pad(np.pad(power, ((0, 1),) * 3, mode="edge"), ((1, 0),) * 3)
        power = sum(
            np.roll(wide, step, dim)[1:-1, 1:-1, 1:-1] for dim in range(3) for step in (1, -1)
        )
        total = total + POLY[m] * power
    return total[:5, :5, :5]


F32 = jnp.float32
VMEM = pl.BlockSpec(memory_space=pltpu.VMEM)
ANYWHERE = pl.BlockSpec(memory_space=pl.ANY)
PARAMS = dict(vmem_limit_bytes=20 * 1024 * 1024)


def partners(axis, sizes):
    dim = AXES.index(axis)
    count, near = sizes[dim], 1 if axis == "gz" else 2
    first, second = [], []
    for at in np.ndindex(*sizes):
        for pairs, other in (
            (first, at[dim] ^ 1),
            (second, at[dim] + 1 if at[dim] % 2 else at[dim] - 1),
        ):
            to = list(at)
            if 0 <= other < count:
                to[dim] = other
            elif sizes[near] > 1:
                to[near] ^= 1
            pairs.append(tuple(int(np.ravel_multi_index(v, sizes)) for v in (at, to)))
    return first, second


def swap(first, second, axis):
    sizes = tuple(lax.axis_size(a) for a in AXES)
    near, far_ones = partners(axis, sizes)
    return lax.ppermute(first, AXES, near), lax.ppermute(second, AXES, far_ones)


def at_end(axis):
    at = lax.axis_index(axis)
    return jnp.logical_or(at == 0, at == lax.axis_size(axis) - 1)


def cleared(axis, value):
    return jnp.where(at_end(axis), 0.0, value)


def is_odd(axis):
    return lax.rem(lax.axis_index(axis), 2) == 1


def cell_coef(density, cell_flags, trim_level):
    trimmed = (1.0 + trim_level.astype(F32)) * 0.2
    share = jnp.where(cell_flags == 1, 1.0, jnp.where(cell_flags == 2, trimmed, 0.001))
    return -3.0 * density * density * density * share


def lane_ids():
    return lax.broadcasted_iota(jnp.int32, (8, LANES), 1)


def row_ids():
    return lax.broadcasted_iota(jnp.int32, (8, LANES), 0)


def half_turn(tile):
    return pltpu.roll(tile, 4, 0)


def rim_tile(first, second, index, odd):
    one = jnp.broadcast_to(first[pl.ds(index, 1), :], (8, LANES))
    two = jnp.broadcast_to(second[pl.ds(index, 1), :], (8, LANES))
    at_top = row_ids() == 0
    return jnp.where(jnp.logical_xor(at_top, odd), one, two)


def two_halves(first, second):
    spare = HALF - first.shape[0]
    if spare:
        zero = jnp.zeros((spare, LANES), F32)
        first = jnp.concatenate([first, zero], axis=0)
        second = jnp.concatenate([second, zero], axis=0)
    return jnp.concatenate([first, second], axis=0).T


def sides_kernel(disp, ys1, ys2):
    _, bx, by, _ = disp.shape
    odd_y = is_odd("gy")
    for c in range(3):
        rows = slice(c * bx, c * bx + bx)
        low, high = disp[c, :, 0, :], disp[c, :, by - 1, :]
        ys1[rows, :] = jnp.where(odd_y, low, high)
        ys2[rows, :] = jnp.where(odd_y, high, low)


def faces_kernel(disp, low, high):
    _, _, by, _ = disp.shape
    n = by // 16
    for c in range(3):
        for y in range(by // 2):
            turned = two_halves(disp[c, :, y, :], disp[c, :, y + by // 2, :])
            low[c * n + y // 8, y % 8 : y % 8 + 1, :] = turned[0:1]
            high[c * n + y // 8, y % 8 : y % 8 + 1, :] = turned[LANES - 1 : LANES]


def ends_kernel(low, high, yr1, yr2_raw, zs1, zs2, yr2):
    odd_z = is_odd("gz")
    n, bx = low.shape[0], yr1.shape[0] // 3
    yr2[...] = cleared("gy", yr2_raw[...])
    zs1[0:n] = jnp.where(odd_z, low[...], high[...])
    zs2[0:n] = jnp.where(odd_z, high[...], low[...])
    zs1[n] = jnp.zeros((8, LANES), F32)
    zs2[n] = jnp.zeros((8, LANES), F32)
    for c in range(3):
        rows = slice(c * bx, c * bx + bx)
        turned = two_halves(yr1[rows, :], yr2[rows, :])
        near, far = turned[0:1], turned[LANES - 1 : LANES]
        zs1[n, c : c + 1, :] = jnp.where(odd_z, near, far)
        zs2[n, c : c + 1, :] = jnp.where(odd_z, far, near)


def x_rows(by):
    tall = by + 8
    planes = 3 * WIDE * tall
    coefs = planes + REACH * by
    return planes, coefs, coefs + 2 * 3 * (by // 16 + 1) * 8


def ends_tiles(by):
    return 3 * (by // 16 + 1)


def outward_kernel(disp, coef, yr1, yr2, zr1, zr2, xs1, xs2, rims):
    _, bx, by, _ = disp.shape
    tall, n = by + 8, by // 16
    odd_x, odd_y, odd_z = is_odd("gx"), is_odd("gy"), is_odd("gz")
    top_row, left = row_ids() == 0, lane_ids() < HALF
    for side in range(2):
        def pick(*at, side=side):
            one, two = zr1[at], cleared("gz", zr2[at])
            return jnp.where(odd_z, two, one) if side else jnp.where(odd_z, one, two)

        for c in range(3):
            base = side * ends_tiles(by) + c * (n + 1)
            for t in range(n):
                rims[base + t] = pick(c * n + t)
            both = jnp.broadcast_to(pick(3 * n, slice(c, c + 1), slice(None)), (8, LANES))
            other = pltpu.roll(both, HALF, 1)
            rims[base + n] = jnp.where(jnp.logical_xor(top_row, odd_y), both, other)
    planes, coefs, _ = x_rows(by)
    for out, at_low in ((xs1, odd_x), (xs2, jnp.logical_not(odd_x))):
        start = jnp.where(at_low, 0, bx - WIDE)
        for c in range(3):
            for k in range(WIDE):
                at = (c * WIDE + k) * tall
                out[at : at + by, :] = disp[c, start + k]
                out[at + by : at + tall, :] = rim_tile(yr1, yr2, c * bx + start + k, odd_y)
        start = jnp.where(at_low, 0, bx - REACH)
        for k in range(REACH):
            out[planes + k * by : planes + (k + 1) * by, :] = coef[start + k]
        for j in range(2 * ends_tiles(by)):
            out[coefs + 8 * j : coefs + 8 * j + 8, :] = rims[j]


def triple(a, b, c):
    ends = a + c
    curve = ends - 2.0 * b
    return 4.0 * b + (2.0 / 3.0) * curve, c - a, curve


def pair(a, b, c):
    return (2.0 / 3.0) * (a + c) + (8.0 / 3.0) * b, c - a


FIELDS = (
    [(0, key) for key in ("MM", "MD", "MS", "DM", "DD", "DS", "SM", "SD")]
    + [(1, key) for key in ("MM", "MD", "DM", "DD", "SM", "SD")]
    + [(2, key) for key in ("MM", "MD", "DM", "DD", "MS", "DS")]
    + [(3, key) for key in ("00", "01", "10", "11")]
)
ALL_THREE = {(0, "MD"), (0, "DM"), (0, "DD"), (1, "DM"), (1, "DD"), (2, "MD"), (2, "DD")}
NO_VALUE = {(0, "MM"), (1, "MM"), (1, "MD"), (2, "MM"), (2, "DM")}


def energy_of(fields):
    grads = {}
    for name, planes in fields.items():
        if name in NO_VALUE or name in ALL_THREE:
            mid, before, after = planes
            curve = after - before
            grads[name + ("D",)], grads[name + ("S",)] = before + after, curve
            if name in ALL_THREE:
                grads[name + ("M",)] = 4.0 * mid + (2.0 / 3.0) * curve
        else:
            grads.update({name + (x,): v for x, v in zip("MD", pair(*planes))})
    names = "MD", "DS"

    def part(c, e, p):
        ops = [names[1 if d == e else 0][p[d]] for d in range(3)]
        return grads[(c, ops[1] + ops[2], ops[0])]

    traces = mixed = shears = None
    for order in (3, 2, 1, 0):
        if traces is not None:
            traces, mixed, shears = (v * (1.0 / 3.0) for v in (traces, mixed, shears))
        for bits in range(8):
            p = (bits >> 2) & 1, (bits >> 1) & 1, bits & 1
            if sum(p) != order:
                continue
            xx, yy, zz = (part(c, c, p) for c in range(3))
            xy = part(0, 1, p) + part(1, 0, p)
            xz = part(0, 2, p) + part(2, 0, p)
            yz = grads[(3, "%d%d" % p[1:], "MD"[p[0]])]
            both = xx + yy
            trace = both + zz
            trace = trace * trace
            mix = xx * yy + both * zz
            shear = xy * xy + xz * xz + yz * yz
            if traces is None:
                traces, mixed, shears = trace, mix, shear
            else:
                traces, mixed, shears = traces + trace, mixed + mix, shears + shear
    scale = 1.0 / 1024.0
    return (
        ((LAMBDA + 2.0 * SHEAR_MODULUS) * scale) * traces
        - (4.0 * SHEAR_MODULUS * scale) * mixed
        + (SHEAR_MODULUS * scale) * shears
    )


def z_pass(tile_of, low_of, high_of, along):
    lane = lane_ids()
    tiles = along.shape[1] // 8 - 1
    for c in range(3):
        for t in range(tiles):
            mid = tile_of(c, t)
            low = jnp.where(lane == 0, low_of(c, t), pltpu.roll(mid, 1, 1))
            high = jnp.where(lane == LANES - 1, high_of(c, t), pltpu.roll(mid, LANES - 1, 1))
            for k, v in enumerate(triple(low, mid, high)):
                along[3 * c + k, 8 * t + 8 : 8 * t + 16, :] = v
                if t == tiles - 1:
                    along[3 * c + k, 0:8, :] = v


def rim_shifts(by, t, spot, to_lane):
    n = by // 16
    if t == 2 * n:
        return n, lax.rem(to_lane + LANES - spot, LANES)
    return t % n, lax.rem(to_lane + 2 * LANES - spot - HALF * (t // n), LANES)


def xy_pass(along, ring, slot, emit, keep=True):
    for t in range(along.shape[1] // 8 - 2):
        rows = slice(8 * t, 8 * t + 8)
        now = {}
        for c in range(3):
            for k, z in enumerate("MDS"):
                three = [along[3 * c + k, 8 * t + 7 + o : 8 * t + 15 + o, :] for o in range(3)]
                values = pair(*three) if z == "S" else triple(*three)
                now.update({(c, y + z): v for y, v in zip("MDS", values)})
        now[(3, "00")] = now[(2, "DM")] + now[(1, "MD")]
        now[(3, "01")] = now[(2, "DD")] + now[(1, "MS")]
        now[(3, "10")] = now[(2, "SM")] + now[(1, "DD")]
        now[(3, "11")] = now[(2, "SD")] + now[(1, "DS")]
        fields = {}
        for f, name in enumerate(FIELDS):
            steps = name in NO_VALUE or name in ALL_THREE
            if steps and keep:
                mid = ring[0, f, rows, :]
                after = now[name] - mid
                if emit is not None:
                    fields[name] = mid, ring[1, f, rows, :], after
                ring[0, f, rows, :] = now[name]
                ring[1, f, rows, :] = after
                continue
            if emit is not None:
                old, mid = ring[slot, f, rows, :], ring[1 - slot, f, rows, :]
                fields[name] = old, mid, now[name]
                if steps:
                    fields[name] = mid, mid - old, now[name] - mid
            ring[slot, f, rows, :] = now[name]
        if emit is not None:
            emit(t, energy_of(fields))


def far(axis, index, size):
    at = lax.axis_index(axis) * size + index
    return jnp.minimum(jnp.minimum(at, lax.axis_size(axis) * size - 1 - at), REACH)


def fill_weights(weights):
    table = reach_weights()
    by = weights.shape[1]
    far_z = far("gz", lane_ids(), LANES)
    for d in range(REACH + 1):
        for t in range(by // 8):
            far_y = far("gy", row_ids() + 8 * t, by)
            value = None
            for j in range(REACH, -1, -1):
                line = jnp.full((8, LANES), table[d, j, REACH], F32)
                for k in range(REACH):
                    line = jnp.where(far_z == k, F32(table[d, j, k]), line)
                value = line if value is None else jnp.where(far_y == j, line, value)
            weights[d, 8 * t : 8 * t + 8, :] = value


def inner_kernel(disp, coef, yr1, yr2, rims, inner, partial, weights, along0, along1, ring):
    _, bx, by, _ = disp.shape
    odd_y = is_odd("gy")
    tiles = by // 8
    fill_weights(weights)

    def along_z(x, along):
        def tile_of(c, t):
            if t < tiles:
                return disp[c, x, 8 * t : 8 * t + 8, :]
            return rim_tile(yr1, yr2, c * bx + x, odd_y)

        def rim(side, to_lane):
            def of(c, t):
                tile, turn = rim_shifts(by, t, x, to_lane)
                return pltpu.roll(rims[side * ends_tiles(by) + c * (by // 16 + 1) + tile], turn, 1)

            return of

        z_pass(tile_of, rim(0, 0), rim(1, LANES - 1), along)

    def across(x, along, slot, total):
        totals = [total]

        def emit(t, energy):
            rows = slice(8 * t, 8 * t + 8)
            value = coef[x - 1, rows, :] * energy
            inner[x - 2, rows, :] = value
            totals.append(totals[-1] + weights[far("gx", x - 1, bx), rows, :] * value)

        xy_pass(along, ring, slot, emit if total is not None else None)
        return totals[-1]

    along_z(0, along0)
    along_z(1, along1)
    across(0, along0, 0, None)
    along_z(2, along0)
    across(1, along1, 1, None)

    def planes_two(k, total):
        along_z(2 * k + 1, along1)
        total = across(2 * k, along0, 0, total)
        along_z(jnp.minimum(2 * k + 2, bx - 1), along0)
        return across(2 * k + 1, along1, 1, total)

    partial[...] = lax.fori_loop(1, bx // 2, planes_two, jnp.zeros((8, LANES), F32))


def outer_kernel(
    disp, coef, yr1, yr2, rims, xr1, xr2, inner, partial, weights,
    source, ys1, ys2, sums_out,
    field, rim_coef, ends, total, sums, along0, along1, ring, sem,
):
    _, bx, by, _ = disp.shape
    cells, tall = bx + 2 * REACH, by + 8
    planes, coefs, _ = x_rows(by)
    count = WIDE + 2
    odd_x, odd_y = is_odd("gx"), is_odd("gy")
    row = row_ids()
    for side in range(2):
        def pick(at, size, side=side):
            one, two = xr1[at : at + size, :], cleared("gx", xr2[at : at + size, :])
            return jnp.where(odd_x, two, one) if side else jnp.where(odd_x, one, two)

        for c in range(3):
            for k in range(WIDE):
                field[side, c, k + 2 * side] = pick((c * WIDE + k) * tall, tall)
            for k in range(2):
                x = bx - 2 + k if side else k
                at = k if side else WIDE + k
                field[side, c, at, 0:by, :] = disp[c, x]
                field[side, c, at, by:tall, :] = rim_tile(yr1, yr2, c * bx + x, odd_y)
        for k in range(REACH):
            rim_coef[side, k + side] = pick(planes + k * by, by)
        rim_coef[side, 0 if side else REACH] = coef[bx - 1 if side else 0]
        for j in range(2 * ends_tiles(by)):
            ends[side, j] = pick(coefs + 8 * j, 8)
    for j in range(2 * ends_tiles(by)):
        ends[2, j] = rims[j]
    total[...] = partial[...]

    def one_side(side, carry):
        high_side = side == 1

        def along_z(i, along):
            low_whose = 2 if i >= WIDE else 0
            low_spot = i - WIDE if i >= WIDE else bx - WIDE + i
            high_whose = 2 if i < 2 else 1
            high_spot = bx - 2 + i if i < 2 else i - 2
            whose = jnp.where(high_side, high_whose, low_whose)
            spot = jnp.where(high_side, high_spot, low_spot)

            def rim(z_side, to_lane):
                def of(c, t):
                    tile, turn = rim_shifts(by, t, spot, to_lane)
                    at = z_side * ends_tiles(by) + c * (by // 16 + 1) + tile
                    return pltpu.roll(ends[whose, at], turn, 1)

                return of

            z_pass(
                lambda c, t: field[side, c, i, 8 * t : 8 * t + 8, :],
                rim(0, 0), rim(1, LANES - 1), along,
            )

        alongs = along0, along1
        along_z(0, along0)
        for i in range(count):
            if i + 1 < count:
                along_z(i + 1, alongs[(i + 1) % 2])

            def emit(t, energy, i=i):
                rows = slice(8 * t, 8 * t + 8)
                value = rim_coef[side, i - 2, rows, :] * energy
                source[side * (cells - WIDE) + i - 2, rows, :] = value
                if i in (2, count - 1):
                    own = high_side if i == 2 else jnp.logical_not(high_side)
                    weight = weights[far("gx", bx - 1 if i == 2 else 0, bx), rows, :]
                    total[...] += jnp.where(own, weight * value, 0.0)

            xy_pass(alongs[i % 2], ring, i % 2, emit if i >= 2 else None, keep=False)
        return carry

    lax.fori_loop(0, 2, one_side, 0)
    sums[...] = jnp.broadcast_to(jnp.sum(total[...], axis=0, keepdims=True), sums.shape)
    leave = pltpu.make_async_copy(sums, sums_out, sem)
    leave.start()


    def copy(x, carry):
        source[x + WIDE] = inner[x]
        return carry

    lax.fori_loop(0, bx - 2, copy, 0, unroll=4)

    def rows_out(q, carry):
        top = row < 4
        first, second = source[2 * q, 0:8, :], source[2 * q + 1, 0:8, :]
        low = jnp.where(top, first, half_turn(second))
        first, second = source[2 * q, by - 8 : by, :], source[2 * q + 1, by - 8 : by, :]
        high = jnp.where(top, half_turn(first), second)
        ys1[q] = jnp.where(odd_y, low, high)
        ys2[q] = jnp.where(odd_y, high, low)
        return carry

    lax.fori_loop(0, cells // 2, rows_out, 0, unroll=6)
    leave.wait()


def pack_columns(source, packed, inside, count):
    cells = source.shape[0]
    top = row_ids() < 4
    for y in range(count):
        tall = jnp.concatenate([source[:, y, :], jnp.zeros((LANES - cells, LANES), F32)], axis=0)
        flat = tall.T
        first, last = flat[0:8], flat[LANES - 8 : LANES]
        packed[y] = jnp.where(top, first, last)
        inside[y] = half_turn(jnp.where(top, last, first))


def pack_kernel(source, both, filtered, *works):
    pack_columns(source, both.at[0], both.at[1], source.shape[1])
    run_sweeps(source, None, filtered, works)


def late_kernel(source, rim, filtered_in, w0, w1, w2, w3, filtered, *works):
    del filtered_in, w0, w1, w2, w3
    run_sweeps(source, rim, filtered, works)


def corner_kernel(yr1, yr2, both, rim, rim_both, zs1, zs2):
    packed, rim_packed, rim_inside = both.at[0], rim_both.at[0], rim_both.at[1]
    by = packed.shape[0]
    odd_y, odd_z = is_odd("gy"), is_odd("gz")
    top = row_ids() < 4

    def unpack(q, carry):
        one, two = yr1[q], cleared("gy", yr2[q])
        high = jnp.where(odd_y, two, one)
        low = jnp.where(odd_y, one, two)
        rim[2 * q] = jnp.where(top, high, half_turn(low))
        rim[2 * q + 1] = jnp.where(top, half_turn(high), low)
        return carry

    lax.fori_loop(0, yr1.shape[0], unpack, 0, unroll=6)
    pack_columns(rim, rim_packed, rim_inside, 8)

    def send(m, first, second):
        low = jnp.where(top, first, half_turn(second))
        high = jnp.where(top, half_turn(first), second)
        zs1[m] = jnp.where(odd_z, low, high)
        zs2[m] = jnp.where(odd_z, high, low)

    for m in range(by // 2):
        send(m, packed[2 * m], packed[2 * m + 1])
    for m in range(4):
        send(by // 2 + m, rim_packed[2 * m], rim_packed[2 * m + 1])


def run_sweeps(source, rim, filtered, works):
    cells, by, _ = source.shape
    bx = cells - 2 * REACH
    tiles = by // 8
    top = row_ids() < 4
    first_x, last_x = lax.axis_index("gx") == 0, lax.axis_index("gx") == lax.axis_size("gx") - 1
    first_y, last_y = lax.axis_index("gy") == 0, lax.axis_index("gy") == lax.axis_size("gy") - 1
    late = rim is not None

    def put(ref, x, t, value):
        ref[x, 8 * t + 8 : 8 * t + 16, :] = value
        if t == tiles:
            ref[x, 0:8, :] = value
        if t == 0:
            ref[x, by + 16 : by + 24, :] = value

    def begin(x, carry):
        if late:
            put(works[0], x, tiles, POLY[4] * rim[x])
        else:
            for t in range(tiles):
                put(works[0], x, t, POLY[4] * source[x, 8 * t : 8 * t + 8, :])
        return carry

    lax.fori_loop(0, cells, begin, 0, unroll=8)
    rim_keep = jnp.logical_not(
        jnp.logical_or(
            jnp.logical_and(last_y, top), jnp.logical_and(first_y, jnp.logical_not(top))
        )
    )
    edge = [0, tiles - 1]
    for k in range(4):
        now = works[k]
        if late:
            here = edge + ([tiles] if k < 3 else [])
        else:
            here = list(range(tiles)) if k < 3 else list(range(1, tiles - 1))

        def sweep(x, k=k, now=now, here=here):
            for t in here:
                at = 8 * t + 8
                mid = now[x, at : at + 8, :]
                value = now[x - 1, at : at + 8, :] + now[x + 1, at : at + 8, :]
                value = value + (now[x, at - 1 : at + 7, :] + now[x, at + 1 : at + 9, :])
                value = value + (pltpu.roll(mid, 1, 1) + pltpu.roll(mid, LANES - 1, 1))
                own = source[x, 8 * t : 8 * t + 8, :] if t < tiles else rim[x]
                value = value + POLY[3 - k] * own
                if k == 3:
                    filtered[x - REACH, 8 * t : 8 * t + 8, :] = value
                else:
                    if t == tiles:
                        value = jnp.where(rim_keep, value, 0.0)
                    put(works[k + 1], x, t, value)

        first, left = (1, cells - 2) if k < 3 else (REACH, bx)
        group = max(g for g in range(2, 36) if left % g == 0)

        def sweeps(j, carry, first=first, group=group, sweep=sweep):
            for g in range(group):
                sweep(first + j * group + g)
            return carry

        lax.fori_loop(0, left // group, sweeps, 0)
        if k < 3:
            later = works[k + 1]

            @pl.when(first_x)
            def _(later=later):
                later[0:REACH] = jnp.zeros((REACH,) + later.shape[1:], F32)

            @pl.when(last_x)
            def _(later=later):
                later[bx + REACH : cells] = jnp.zeros((REACH,) + later.shape[1:], F32)


def strip_kernel(both, rim_both, zr1, zr2, strip):
    by = both.shape[1]
    tall = by + 8
    packed, inside, rim_packed, rim_inside = both.at[0], both.at[1], rim_both.at[0], rim_both.at[1]
    odd_z, top = is_odd("gz"), row_ids() < 4
    for m in range(tall // 2):
        one, two = zr1[m], cleared("gz", zr2[m])
        low = jnp.where(odd_z, one, two)
        high = jnp.where(odd_z, two, one)
        for part in range(2):
            y = 2 * m + part
            own = half_turn(packed[y] if y < by else rim_packed[y - by])
            strip[y, 0] = jnp.where(top, half_turn(low) if part else low, own)
            strip[y, 1] = jnp.where(top, own, high if part else half_turn(high))
            strip[y, 2] = inside[y] if y < by else rim_inside[y - by]


def finish_kernel(
    count, inner, strip, density, sums,
    projected_out, filtered_out, work0, work1, edges, projected, filtered, sems,
):
    bx, by, _ = density.shape
    tall = by + 8
    lane, row = lane_ids(), row_ids()
    top = row < 4
    first_x, last_x = lax.axis_index("gx") == 0, lax.axis_index("gx") == lax.axis_size("gx") - 1
    first_y, last_y = lax.axis_index("gy") == 0, lax.axis_index("gy") == lax.axis_size("gy") - 1
    first_z, last_z = lax.axis_index("gz") == 0, lax.axis_index("gz") == lax.axis_size("gz") - 1

    inside_x = jnp.logical_not(
        jnp.logical_or(
            jnp.logical_and(first_x, lane < REACH),
            jnp.logical_and(last_x, lane >= bx + REACH),
        )
    )
    keeps = (
        jnp.logical_and(inside_x, jnp.logical_not(jnp.logical_and(first_z, top))),
        jnp.logical_and(
            inside_x, jnp.logical_not(jnp.logical_and(last_z, jnp.logical_not(top)))
        ),
        inside_x,
    )
    work0[...] = POLY[4] * strip[...]
    for k in range(4):
        now, later = (work0, work1)[k % 2], (work0, work1)[(k + 1) % 2]
        for y in range(tall if k < 3 else by):
            low, high, mid = (now[y, part] for part in range(3))
            ups = (
                jnp.where(row == 7, pltpu.roll(mid, 7, 0), pltpu.roll(low, 7, 0)),
                pltpu.roll(high, 7, 0),
                jnp.where(row == 7, pltpu.roll(high, 7, 0), pltpu.roll(mid, 7, 0)),
            )
            downs = (
                pltpu.roll(low, 1, 0),
                jnp.where(row == 0, pltpu.roll(mid, 1, 0), pltpu.roll(high, 1, 0)),
                jnp.where(row == 0, pltpu.roll(low, 1, 0), pltpu.roll(mid, 1, 0)),
            )
            for part in range(3 if k < 3 else 2):
                tile = now[y, part]
                value = now[(y + 1) % tall, part] + now[(y - 1) % tall, part]
                value = value + (pltpu.roll(tile, 1, 1) + pltpu.roll(tile, LANES - 1, 1))
                value = value + (ups[part] + downs[part])
                value = value + POLY[3 - k] * strip[y, part]
                keep = keeps[part]
                if y >= by:
                    outside = first_y if y >= by + 4 else last_y
                    keep = jnp.logical_and(keep, jnp.logical_not(outside))
                later[y, part] = jnp.where(keep, value, 0.0)

    blank = jnp.zeros((LANES - 16, LANES), F32)
    for y in range(by):
        first = half_turn(work0[y, 0])
        last = half_turn(work0[y, 1])
        turned = jnp.concatenate([first, blank, last], axis=0).T
        edges[:, y, :] = turned[0 : bx + 8, :]

    scale = jnp.full((8, LANES), -jnp.sum(sums[...]) / count, F32) + 1e-06
    inverse = 1.0 / scale
    lower = math.tanh(SHARPNESS * THRESHOLD)
    bottom = 1.0 / (lower + math.tanh(SHARPNESS * (1.0 - THRESHOLD)))
    at_face = jnp.logical_or(lane < REACH, lane >= LANES - REACH)

    def project(x, carry):
        for t in range(by // 8):
            rows = slice(8 * t, 8 * t + 8)
            value = jnp.where(at_face, edges[x + REACH, rows, :], inner[x, rows, :])
            filtered[x, rows, :] = value
            trial = density[x, rows, :] - STEP_SIZE * (value * inverse + 1.0)
            level = lower + jnp.tanh(SHARPNESS * (trial - THRESHOLD))
            projected[x, rows, :] = level * bottom
        return carry

    chunks = 4
    size = bx // chunks

    def leave(j):
        at = pl.ds(j * size, size)
        return [
            pltpu.make_async_copy(here.at[at], there.at[at], sems.at[i, j])
            for i, (here, there) in enumerate(
                ((projected, projected_out), (filtered, filtered_out))
            )
        ]

    for j in range(chunks):
        lax.fori_loop(j * size, (j + 1) * size, project, 0, unroll=8)
        for copy in leave(j):
            copy.start()
    for j in range(chunks):
        for copy in leave(j):
            copy.wait()


def call(kernel, outs, scratch=(), cost=0, placed=None, aliases=None):
    return pl.pallas_call(
        kernel,
        out_shape=[jax.ShapeDtypeStruct(s, F32) for s in outs],
        out_specs=placed or [VMEM] * len(outs),
        input_output_aliases=aliases or {},
        scratch_shapes=[pltpu.VMEM(s, F32) if isinstance(s, tuple) else s for s in scratch],
        compiler_params=pltpu.CompilerParams(**PARAMS),
        cost_estimate=pl.CostEstimate(flops=cost, bytes_accessed=cost, transcendentals=0),
    )


def body(displacement, density, cell_flags, trim_level):
    bx, by, bz = density.shape
    assert bz == LANES and bx <= HALF and bx % 2 == 0 and by % 16 == 0
    cells, tall = bx + 2 * REACH, by + 8
    devices = lax.axis_size(AXES)
    ys1, ys2 = call(sides_kernel, [(3 * bx, LANES)] * 2)(displacement)
    yr1, yr2 = swap(ys1, ys2, "gy")
    n = 3 * (by // 16)
    low, high = call(faces_kernel, [(n, 8, LANES)] * 2, cost=6_000_000)(displacement)
    flags_here, low = lax.optimization_barrier((cell_flags, low))
    coef = cell_coef(density, flags_here, trim_level)
    coef, low = lax.optimization_barrier((coef, low))
    zs1, zs2, yr2 = call(ends_kernel, [(n + 1, 8, LANES)] * 2 + [(3 * bx, LANES)])(
        low, high, yr1, yr2
    )
    zr1, zr2 = swap(zs1, zs2, "gz")
    brick = (bx, by, LANES)
    rows = x_rows(by)[2]
    xs1, xs2, rims = call(
        outward_kernel, [(rows, LANES), (rows, LANES), (2 * ends_tiles(by), 8, LANES)]
    )(displacement, coef, yr1, yr2, zr1, zr2)
    xr1, xr2 = swap(xs1, xs2, "gx")
    along = (9, by + 16, LANES)
    ring = (2, 24, by, LANES)
    inner, partial, weights = call(
        inner_kernel,
        [(bx - 2, by, LANES), (8, LANES), (REACH + 1, by, LANES)],
        [along, along, ring],
        cost=60_000_000,
    )(displacement, coef, yr1, yr2, rims)
    source, ys1, ys2, sums = call(
        outer_kernel,
        [
            (cells, by, LANES),
            (cells // 2, 8, LANES),
            (cells // 2, 8, LANES),
            (devices, LANES),
        ],
        [
            (2, 3, WIDE + 2, tall, LANES),
            (2, REACH + 1, by, LANES),
            (3, 2 * ends_tiles(by), 8, LANES),
            (8, LANES),
            (devices, LANES),
            along,
            along,
            ring,
            pltpu.SemaphoreType.DMA,
        ],
        placed=[VMEM] * 3 + [ANYWHERE],
    )(displacement, coef, yr1, yr2, rims, xr1, xr2, inner, partial, weights)
    yr1, yr2 = swap(ys1, ys2, "gy")
    work = [(cells, by + 24, LANES)] * 4
    both, *early = call(pack_kernel, [(2, by, 8, LANES), brick] + work, cost=20_000_000)(source)
    sums = lax.all_to_all(sums, AXES, split_axis=0, concat_axis=0, tiled=True)
    rim, rim_both, zs1, zs2 = call(
        corner_kernel,
        [
            (cells, 8, LANES),
            (2, 8, 8, LANES),
            (tall // 2, 8, LANES),
            (tall // 2, 8, LANES),
        ],
    )(yr1, yr2, both)
    zr1, zr2 = swap(zs1, zs2, "gz")
    middle = call(
        late_kernel,
        [brick] + work,
        cost=20_000_000,
        aliases={i + 2: i for i in range(5)},
    )(source, rim, *early)[0]
    strip_shape = (tall, 3, 8, LANES)
    (strip,) = call(strip_kernel, [strip_shape])(both, rim_both, zr1, zr2)
    return call(
        functools.partial(finish_kernel, float(bx * by * bz * devices)),
        [brick, brick],
        [
            strip_shape,
            strip_shape,
            (bx + 8, by, LANES),
            brick,
            brick,
            pltpu.SemaphoreType.DMA((2, 4)),
        ],
        placed=[ANYWHERE] * 2,
    )(middle, strip, density, sums)


def solution(mesh):
    return jax.shard_map(
        body,
        mesh=mesh,
        in_specs=(P(None, *AXES), P(*AXES), P(*AXES), P(*AXES)),
        out_specs=(P(*AXES), P(*AXES)),
        check_vma=False,
    )
```
